32 devices in a mesh: prow: 4 (over y, x), pcol: 8 (over z, core).
Axes of the slice: x: 2, y: 2, z: 4, core: 2. Of those that a mesh axis runs over, the one named last changes fastest.
Arguments:
- window: float32 [20480, 20480], P('prow', 'pcol'), as said below
- pattern: int32 [160, 160], P('prow', 'pcol'), may hold values from 0 to 1, as said below
- row_lists: int32 [2, 2, 64], replicated, may hold values from 0 to 159, as said below
- factor: float32 [2, 20480, 256], P(None, 'prow', 'pcol'), may hold values from -0.5 to 0.5
- diag_inverse: float32 [2, 128, 256], replicated, as said below
Outputs:
- panels: float32 [2, 20480, 256], P(None, 'pcol', 'prow')
- diagonals: float32 [2, 128, 256], P(None, None, 'prow')
The draws below stay inside these ranges and needn't reach their ends.
Inputs may be any that keep to these rules, and one draw needn't show every extreme that they name: `pattern`: Symmetric; every diagonal block is stored; about 85 in 100 blocks are stored. `row_lists`: each list names distinct blocks. The lists of level 0 never name blocks 160 - 2 and 159; list s of level 1 is the first 62 entries of list s of level 0 followed by 160 - 2 and 159. `window`: exactly symmetric. `diag_inverse`: each of the two 128 x 128 blocks of a level is symmetric up to rounding.
All inputs are finite; a program needn't handle non-finite values.
Results may differ from the reference program's by a relative error of at most 0.00011.
Values sent between devices are 32-bit elements; how exact they have to be, the bound alone decides.
No kernel may reach another device: no remote copies, remote signals or barrier semaphores. Data moves between devices by JAX's collectives and lax.ppermute only.
A program may use at most 256 MiB of HBM per device.

```python
import jax
import jax.numpy as jnp
from jax import lax

BS = 128
NB = 160
RS = 64
ROWS = 20480


def draw_window(key, part):
    total_rows = NB * BS
    base = jax.random.normal(key, (total_rows, total_rows), jnp.float32)
    symmetric = (base + base.T) * 0.70710678
    return symmetric * (0.85 * RS) ** (-0.5)


def draw_pattern(key, part):
    numbers = jax.random.randint(key, (NB, NB), 0, 100)
    stored = (numbers < 85).astype(jnp.int32)
    symmetric = jnp.triu(stored) + jnp.triu(stored, 1).T
    return jnp.maximum(symmetric, jnp.eye(NB, dtype=jnp.int32)).astype(jnp.int32)


def draw_row_lists(key, part):
    first_level = []
    second_level = []
    for node_index in range(2):
        subkey = jax.random.fold_in(key, 11 + node_index)
        shuffled = jax.random.permutation(subkey, NB - 2).astype(jnp.int32)
        listed = shuffled[:RS]
        first_level.append(listed)
        second_level.append(jnp.concatenate([listed[:RS - 2], jnp.array([NB - 2, NB - 1], dtype=jnp.int32)]))
    return jnp.stack([jnp.stack(first_level), jnp.stack(second_level)]).astype(jnp.int32)


def draw_diag_inverse(key, part):
    base = 2.0 * jax.random.normal(key, (2, 2, BS, BS), jnp.float32)
    symmetric = (base + jnp.swapaxes(base, 2, 3)) * 0.70710678
    return jnp.concatenate([symmetric[:, 0], symmetric[:, 1]], axis=2)


def levels(own_key, dims, pieces, least, largest):
    loudness = 1.0
    for axis_at, parts in pieces:
        draws = jax.random.uniform(jax.random.fold_in(jax.random.fold_in(own_key, 6), axis_at), (parts,), jnp.float32, least / len(pieces), largest / len(pieces))
        loudness = loudness * jnp.repeat(jnp.exp(draws), dims[axis_at] // parts).reshape((-1,) + (1,) * (len(dims) - 1 - axis_at))
    return loudness


def noise(own_key, extent, scale, reach, cuts=(), kind=jnp.bfloat16):
    drawn = jax.random.normal(own_key, extent, jnp.float32) * scale
    if len(cuts) > 0:
        drawn = levels(own_key, extent, cuts, -0.22, 0.18) * drawn
    return jnp.clip(drawn, min=-reach, max=reach).astype(kind)


def setup_inputs(seed: int = 0) -> dict:
    seeds = jax.random.split(jax.random.key(seed), 6)
    window = draw_window(jax.random.fold_in(seeds[5], 71), 0)
    pattern = draw_pattern(jax.random.fold_in(seeds[5], 71), 0)
    row_lists = draw_row_lists(jax.random.fold_in(seeds[5], 71), 0)
    factor = noise(seeds[3], (2, ROWS, 2 * BS), BS ** -0.5, 0.5, ((1, 4), (2, 8)), jnp.float32)
    diag_inverse = draw_diag_inverse(jax.random.fold_in(seeds[5], 71), 0)
    return dict(window=window, pattern=pattern, row_lists=row_lists, factor=factor, diag_inverse=diag_inverse)


exact_mode = lax.Precision.HIGHEST


def block_flags(index_lists):
    blocks = jnp.arange(NB, dtype=jnp.int32)
    return jnp.any(blocks[None, :, None] == index_lists[:, None, :], axis=-1).astype(jnp.float32)


def cell_mask(index_lists):
    flags = jnp.repeat(block_flags(index_lists), BS, axis=1)
    first_half = jnp.broadcast_to(flags[0][:, None], (NB * BS, BS))
    second_half = jnp.broadcast_to(flags[1][:, None], (NB * BS, BS))
    return jnp.concatenate([first_half, second_half], axis=1)


def window_product(window, pattern, factor_panel):
    blocks = jnp.arange(NB, dtype=jnp.int32)
    usable = (blocks < NB - 2).astype(jnp.float32)
    keeper = pattern.astype(jnp.float32) * usable[:, None] * usable[None, :]
    strips = window.reshape(NB, BS, NB * BS)

    def one_strip(inputs):
        strip_rows, keep_row = inputs
        masked = (strip_rows.reshape(BS, NB, BS) * keep_row[None, :, None]).reshape(BS, NB * BS)
        return jnp.dot(masked, factor_panel, precision=exact_mode, preferred_element_type=jnp.float32)

    return lax.map(one_strip, (strips, keeper)).reshape(NB * BS, 2 * BS)


def diag_block(live_factor, solved, inverse_part):
    gram_first = jnp.dot(live_factor[:, :BS].T, solved[:, :BS], precision=exact_mode, preferred_element_type=jnp.float32)
    gram_second = jnp.dot(live_factor[:, BS:].T, solved[:, BS:], precision=exact_mode, preferred_element_type=jnp.float32)
    return inverse_part - jnp.concatenate([gram_first, gram_second], axis=1)


def reference(window, pattern, row_lists, factor, diag_inverse):
    total_rows = NB * BS
    mask_one = cell_mask(row_lists[0])
    live_one = factor[0] * mask_one
    image_one = window_product(window, pattern, live_one)
    solved_one = -(mask_one * image_one)
    diag_one = diag_block(live_one, solved_one, diag_inverse[0])
    mask_two = cell_mask(row_lists[1])
    live_two = factor[1] * mask_two
    image_two = window_product(window, pattern, live_two)
    slot_rows = live_two[total_rows - 2 * BS:]
    image_two = image_two + jnp.dot(solved_one, slot_rows, precision=exact_mode, preferred_element_type=jnp.float32)
    corner = jnp.dot(solved_one.T, live_two, precision=exact_mode, preferred_element_type=jnp.float32)
    corner = corner + jnp.concatenate([
        jnp.dot(diag_one[:, :BS], slot_rows[:BS], precision=exact_mode, preferred_element_type=jnp.float32),
        jnp.dot(diag_one[:, BS:], slot_rows[BS:], precision=exact_mode, preferred_element_type=jnp.float32)], axis=0)
    image_two = jnp.concatenate([image_two[:total_rows - 2 * BS], image_two[total_rows - 2 * BS:] + corner], axis=0)
    solved_two = -(mask_two * image_two)
    diag_two = diag_block(live_two, solved_two, diag_inverse[1])
    return jnp.stack([solved_one, solved_two]), jnp.stack([diag_one, diag_two])
```

```python
import functools

import jax
import jax.numpy as jnp
from jax import lax
from jax.experimental import pallas as pl
from jax.experimental.pallas import tpu as pltpu
from jax.sharding import PartitionSpec as P

BS = 128
DEPTH = 4
VMEM_BYTES = 60 * 1024 * 1024

F32 = jnp.float32
BF16 = jnp.bfloat16
exact_mode = lax.Precision.HIGHEST


class Sizes:
    def __init__(self, rows, cols, thin, prow, pcol, listed, row_cap, col_cap):
        self.prow, self.pcol, self.planes = prow, pcol, pcol // 2
        self.thin, self.listed = thin, listed
        self.rows = rows
        self.row_blocks, self.col_blocks = rows // BS, cols // BS
        self.row_cap, self.col_cap = row_cap, col_cap
        self.deep = -(-row_cap // DEPTH) * DEPTH
        self.wide = (row_cap + 1) * BS
        self.slot = col_cap // prow
        self.lanes = self.slot * BS
        self.piece = 2 * BS // prow
        self.half = pcol // 2
        at = 0
        for name, extent in (
            ("at_rows", 2 * (self.deep + 1)),
            ("at_cols", 2 * (col_cap + 1)),
            ("at_seat", 2 * (col_cap + 1)),
            ("at_second", 2 * (col_cap + 1)),
            ("at_place", 2 * self.col_blocks),
            ("at_count", 5),
        ):
            setattr(self, name, at)
            at += extent
        self.plan = at


def plan_body(z, ids, lists, thin_ref, plan, own, member, seat):
    p, j = ids[0], ids[1]
    blocks = z.row_blocks * z.prow

    def clear(k, c):
        member[k] = 0
        return c

    lax.fori_loop(0, blocks, clear, 0)

    def blank(k, c):
        plan[k] = 0
        return c

    lax.fori_loop(0, z.at_seat, blank, 0)
    for s in range(2):
        def unseat(k, c, s=s):
            plan[z.at_seat + s * (z.col_cap + 1) + k] = -1
            plan[z.at_second + s * (z.col_cap + 1) + k] = 0
            return c

        lax.fori_loop(0, z.col_cap + 1, unseat, 0)
        for level in range(2):
            def mark(k, c, s=s, level=level):
                b = lists[(level * 2 + s) * z.listed + k]
                member[b] = member[b] | (1 << (2 * level + s))
                return c

            lax.fori_loop(0, z.listed, mark, 0)

    def take_row(r, counts):
        v = member[p * z.row_blocks + r]
        result = []
        for s in range(2):
            plan[z.at_rows + s * (z.deep + 1) + counts[s]] = r
            held = (v >> s) & 1
            seat[s * z.row_blocks + r] = jnp.where(held == 1, counts[s], -1)
            result.append(counts[s] + held)
        return tuple(result)

    row_counts = lax.fori_loop(0, z.row_blocks, take_row, (0, 0))

    def put_col(s, t, cb, v):
        base = s * (z.col_cap + 1) + t
        plan[z.at_cols + base] = cb
        plan[z.at_second + base] = (v >> (2 + s)) & 1
        r = j * z.col_blocks + cb - p * z.row_blocks
        inside = jnp.logical_and(r >= 0, r < z.row_blocks)
        safe = jnp.clip(r, 0, z.row_blocks - 1)
        plan[z.at_seat + base] = jnp.where(inside, seat[s * z.row_blocks + safe], -1)
        plan[z.at_place + s * z.col_blocks + cb] = t

    def take_both(cb, count):
        v = member[j * z.col_blocks + cb]
        for s in range(2):
            plan[z.at_place + s * z.col_blocks + cb] = -1
        both = (v & 3) == 3

        @pl.when(both)
        def _():
            for s in range(2):
                put_col(s, count, cb, v)

        return count + both.astype(jnp.int32)

    common = lax.fori_loop(0, z.col_blocks, take_both, 0)

    def take_one(cb, counts):
        v = member[j * z.col_blocks + cb]
        result = []
        for s in range(2):
            single = (v & 3) == (1 << s)

            @pl.when(single)
            def _(s=s):
                put_col(s, counts[s], cb, v)

            result.append(counts[s] + single.astype(jnp.int32))
        return tuple(result)

    col_counts = lax.fori_loop(0, z.col_blocks, take_one, (common, common))
    for k, value in enumerate(row_counts + col_counts + (common,)):
        plan[z.at_count + k] = value

    mine = 2 * j // z.pcol

    def pack(k, c):
        r = plan[z.at_rows + mine * (z.deep + 1) + k]
        held = k < plan[z.at_count + mine]
        second = jnp.logical_and(held, ((member[p * z.row_blocks + r] >> (2 + mine)) & 1) == 1)
        source = pl.ds(pl.multiple_of(r * BS, BS), BS)
        target = pl.ds(pl.multiple_of(k * BS, BS), BS)
        own[0, :, target] = jnp.where(held, thin_ref[0, :, source], 0.0)
        own[1, :, target] = jnp.where(second, thin_ref[1, :, source], 0.0)
        return c

    lax.fori_loop(0, z.row_cap, pack, 0)
    for q in range(2):
        own[q, :, z.row_cap * BS :] = thin_ref[1, :, z.rows - (2 - q) * BS : z.rows - (1 - q) * BS]


def make_plan(z, ids, lists, thin_factor):
    smem = pl.BlockSpec(memory_space=pltpu.SMEM)
    vmem = pl.BlockSpec(memory_space=pltpu.VMEM)
    return pl.pallas_call(
        functools.partial(plan_body, z),
        out_shape=(
            jax.ShapeDtypeStruct((z.plan,), jnp.int32),
            jax.ShapeDtypeStruct((2, z.thin, z.wide), F32),
        ),
        in_specs=[smem, smem, vmem],
        out_specs=(smem, vmem),
        scratch_shapes=[
            pltpu.SMEM((z.row_blocks * z.prow,), jnp.int32),
            pltpu.SMEM((2 * z.row_blocks,), jnp.int32),
        ],
        compiler_params=pltpu.CompilerParams(vmem_limit_bytes=VMEM_BYTES),
        name="plan_rows",
    )(ids, lists, thin_factor)


def pack_body(z, plan, pattern, place, strip, high, low):
    k = pl.program_id(0)
    s = place[0]
    row_held = k < plan[z.at_count + s]
    r = plan[z.at_rows + s * (z.deep + 1) + k]
    cols = plan[z.at_count + 2 + s]
    for t in range(z.col_cap):
        span = slice(t * BS, (t + 1) * BS)
        cb = plan[z.at_cols + s * (z.col_cap + 1) + t]
        keep = jnp.logical_and(
            jnp.logical_and(row_held, t < cols), pattern[r * z.col_blocks + cb] > 0
        )

        @pl.when(keep)
        def _():
            block = strip[:, pl.ds(pl.multiple_of(cb * BS, BS), BS)]
            top = block.astype(BF16)
            high[:, span] = top
            low[:, span] = (block - top.astype(F32)).astype(BF16)

        @pl.when(jnp.logical_not(keep))
        def _():
            high[:, span] = jnp.zeros((BS, BS), BF16)
            low[:, span] = jnp.zeros((BS, BS), BF16)


def pack_window(z, plan, pattern, place, window):
    def strip_at(k, plan, pattern, place):
        s = place[0]
        last = jnp.maximum(plan[z.at_count + s] - 1, 0)
        return plan[z.at_rows + s * (z.deep + 1) + jnp.minimum(k, last)], 0

    kept = pl.BlockSpec((BS, z.col_cap * BS), lambda k, *_: (k, 0))
    shape = jax.ShapeDtypeStruct((z.deep * BS, z.col_cap * BS), BF16)
    return pl.pallas_call(
        functools.partial(pack_body, z),
        out_shape=(shape, shape),
        grid_spec=pltpu.PrefetchScalarGridSpec(
            num_scalar_prefetch=3,
            grid=(z.deep,),
            in_specs=[pl.BlockSpec((BS, z.col_blocks * BS), strip_at)],
            out_specs=(kept, kept),
        ),
        compiler_params=pltpu.CompilerParams(vmem_limit_bytes=VMEM_BYTES),
        cost_estimate=pl.CostEstimate(
            flops=0, transcendentals=0, bytes_accessed=z.deep * BS * z.col_blocks * BS * 6
        ),
        name="pack_window",
    )(plan, pattern, place, window)


def product_body(z, reach, plan, place, *refs):
    names = [(0, 0)] if 0 in reach else []
    for d in reach:
        if d > 0:
            names += [(-d, 0), (d, 0)]
    sources = {}
    count = 2 * len(names)
    for k, (step, _) in enumerate(names):
        sources[step] = (refs[2 * k], refs[2 * k + 1])
    high, low = refs[count], refs[count + 1]
    sums = refs[count + 2 : count + 2 + z.prow]
    seats = refs[count + 2 + z.prow : count + 2 + 2 * z.prow]
    tail = refs[count + 2 + 2 * z.prow]
    raw, top, rest, total, chosen, sems = refs[count + 3 + 2 * z.prow :]
    g = pl.program_id(0)
    s, plane, core, p = place[0], place[1], place[2], place[3]
    per = z.planes // 2

    @pl.when(g == 0)
    def _():
        for qi in range(per):
            away = s * per + qi - plane
            for c in range(2):
                slot = qi * 2 + c
                for step, pair in sources.items():
                    for k in range(2):
                        @pl.when(jnp.logical_and(away == step, (c == core) == (k == 0)))
                        def _(pair=pair, k=k, slot=slot):
                            pltpu.make_async_copy(pair[k], raw.at[slot], sems.at[slot]).start()
        any_source = next(iter(sources.values()))[0]
        for slot in range(z.half):
            pltpu.make_async_copy(any_source, raw.at[slot], sems.at[slot]).wait()
            for level in range(2):
                rows = slice(level * BS + slot * z.thin, level * BS + (slot + 1) * z.thin)
                value = raw[slot, level, :, : z.row_cap * BS]
                head = value.astype(BF16)
                top[rows, : z.row_cap * BS] = head
                rest[rows, : z.row_cap * BS] = (value - head.astype(F32)).astype(BF16)
                if z.deep > z.row_cap:
                    blank = jnp.zeros((z.thin, (z.deep - z.row_cap) * BS), BF16)
                    top[rows, z.row_cap * BS :] = blank
                    rest[rows, z.row_cap * BS :] = blank
                tail[slot * z.thin : (slot + 1) * z.thin, level * BS : (level + 1) * BS] = jnp.where(
                    p == z.prow - 1, raw[slot, level, :, z.row_cap * BS :], 0.0
                )

    i = g ^ p
    total[...] = jnp.zeros_like(total)
    cols = plan[z.at_count + 2 + s]
    steps = jnp.where(i * z.slot < cols, (plan[z.at_count + s] + DEPTH - 1) // DEPTH, 0)

    def step(k, c):
        span = pl.ds(pl.multiple_of(k * DEPTH * BS, DEPTH * BS), DEPTH * BS)
        x_top, x_rest = top[:, span], rest[:, span]
        w_top, w_rest = high[span, :], low[span, :]
        total[...] += (
            jnp.dot(x_top, w_rest, preferred_element_type=F32)
            + jnp.dot(x_rest, w_top, preferred_element_type=F32)
            + jnp.dot(x_top, w_top, preferred_element_type=F32)
        )
        return c

    lax.fori_loop(0, steps, step, 0)
    for t in range(z.slot):
        at = plan[z.at_seat + s * (z.col_cap + 1) + i * z.slot + t]
        span = slice(t * BS, (t + 1) * BS)
        safe = pl.ds(pl.multiple_of(jnp.maximum(at, 0) * BS, BS), BS)
        for slot in range(z.half):
            for level in range(2):
                rows = slice(level * BS + slot * z.thin, level * BS + (slot + 1) * z.thin)
                chosen[rows, span] = jnp.where(at >= 0, raw[slot, level, :, safe], 0.0)
    for gg in range(z.prow):
        @pl.when(g == gg)
        def _(gg=gg):
            sums[gg][...] = total[...]
            seats[gg][...] = chosen[...]


def product(z, reach, plan, place, streams, packed):
    arrays = []
    if 0 in reach:
        arrays += list(streams[0])
    for d in reach:
        if d > 0:
            arrays += list(streams[-d]) + list(streams[d])
    anywhere = pl.BlockSpec(memory_space=pl.ANY)
    strip = pl.BlockSpec((z.deep * BS, z.lanes), lambda g, plan, place: (0, g ^ place[3]))
    whole = pl.BlockSpec((2 * BS, z.lanes), lambda g, *_: (0, 0))
    shape = jax.ShapeDtypeStruct((2 * BS, z.lanes), F32)
    out = pl.pallas_call(
        functools.partial(product_body, z, reach),
        out_shape=(shape,) * (2 * z.prow) + (jax.ShapeDtypeStruct((BS, 2 * BS), F32),),
        grid_spec=pltpu.PrefetchScalarGridSpec(
            num_scalar_prefetch=2,
            grid=(z.prow,),
            in_specs=[anywhere] * len(arrays) + [strip, strip],
            out_specs=(whole,) * (2 * z.prow) + (pl.BlockSpec((BS, 2 * BS), lambda g, *_: (0, 0)),),
            scratch_shapes=[
                pltpu.VMEM((z.half, 2, z.thin, z.wide), F32),
                pltpu.VMEM((2 * BS, z.deep * BS), BF16),
                pltpu.VMEM((2 * BS, z.deep * BS), BF16),
                pltpu.VMEM((2 * BS, z.lanes), F32),
                pltpu.VMEM((2 * BS, z.lanes), F32),
                pltpu.SemaphoreType.DMA((z.half,)),
            ],
        ),
        compiler_params=pltpu.CompilerParams(vmem_limit_bytes=VMEM_BYTES),
        cost_estimate=pl.CostEstimate(
            flops=6 * 2 * BS * z.row_cap * BS * z.col_cap * BS,
            transcendentals=0,
            bytes_accessed=z.deep * BS * z.col_cap * BS * 4,
        ),
        name="window_product",
    )(plan, place, *arrays, *packed)
    return out[: z.prow], out[z.prow : 2 * z.prow], out[2 * z.prow]


def plain(left, right):
    return jnp.dot(left, right, precision=exact_mode, preferred_element_type=F32)


def across(left, right):
    return lax.dot_general(
        left, right, (((1,), (1,)), ((), ())), precision=exact_mode, preferred_element_type=F32
    )


def finish_body(z, plan, place, *refs):
    n = z.prow
    near_sum, far_sum = refs[:n], refs[n : 2 * n]
    near_seat, far_seat = refs[2 * n : 3 * n], refs[3 * n : 4 * n]
    near_tail, far_tail = refs[4 * n : 5 * n], refs[5 * n : 6 * n]
    corners = refs[6 * n]
    outs = refs[6 * n + 1 : 7 * n + 1]
    image, live, tails, done, small = refs[7 * n + 1 :]
    near, p, first = place[0], place[3], place[4]
    for s, sums, seats, ends in (
        (near, near_sum, near_seat, near_tail),
        (1 - near, far_sum, far_seat, far_tail),
    ):
        image[s] = functools.reduce(lambda a, b: a + b, [r[...] for r in sums])
        live[s] = functools.reduce(lambda a, b: a + b, [r[...] for r in seats])
        tails[pl.ds(pl.multiple_of(s * BS, BS), BS), :] = functools.reduce(
            lambda a, b: a + b, [r[...] for r in ends]
        )
    lane = lax.broadcasted_iota(jnp.int32, (1, z.lanes), 1) // BS + p * z.slot
    shared = lane < plan[z.at_count + 4]
    for s in range(2):
        other = 1 - s
        keep = jnp.zeros((1, z.lanes), F32)
        for t in range(z.slot):
            flag = plan[z.at_second + s * (z.col_cap + 1) + p * z.slot + t].astype(F32)
            keep = jnp.where(lane == p * z.slot + t, flag, keep)
        own_first = image[s, :BS, :]
        other_first = jnp.where(shared, image[other, :BS, :], 0.0)
        tail = tails[s * BS : (s + 1) * BS, :]
        second = (
            image[s, BS:, :]
            - plain(tail[:, s * BS : (s + 1) * BS], own_first)
            - plain(tail[:, other * BS : (other + 1) * BS], other_first)
        )
        done[s, 0] = -own_first
        done[s, 1] = -(second * keep)
        live_second = live[s, BS:, :]
        started = jnp.where(first == 1, 1.0, 0.0)
        gram = across(own_first, live[s, :BS, :]) + started * corners[0, :, s * BS : (s + 1) * BS].T
        small[s * BS : (s + 1) * BS, :BS] = gram
        small[s * BS : (s + 1) * BS, BS : 2 * BS] = (
            across(second, live_second) + started * corners[1, :, s * BS : (s + 1) * BS].T
        )
        block = slice(2 * BS + s * BS, 2 * BS + (s + 1) * BS)
        crossed = plain(tails[:, s * BS : (s + 1) * BS], gram)
        small[s * BS : (s + 1) * BS, block] = crossed[s * BS : (s + 1) * BS] - across(live_second, own_first)
        small[other * BS : (other + 1) * BS, block] = crossed[other * BS : (other + 1) * BS] - across(
            jnp.where(shared, live[other, BS:, :], 0.0), own_first
        )
    for s in range(2):
        rows = slice(s * BS, (s + 1) * BS)
        small[rows, BS : 2 * BS] += across(small[rows, 2 * BS :], tails[rows, :])
    per = n // 2
    for d in range(n):
        q = p ^ d
        s, h = q // per, q % per
        for level in range(2):
            outs[d][level, :, : z.lanes] = done[s, level, pl.ds(pl.multiple_of(h * z.piece, z.piece), z.piece), :]
            outs[d][level, :, z.lanes :] = small[
                pl.ds(pl.multiple_of(q * z.piece, z.piece), z.piece), level * 2 * BS : (level + 1) * 2 * BS
            ]


def finish(z, plan, place, arrays, corners):
    smem = pl.BlockSpec(memory_space=pltpu.SMEM)
    vmem = pl.BlockSpec(memory_space=pltpu.VMEM)
    shape = jax.ShapeDtypeStruct((2, z.piece, z.lanes + 2 * BS), F32)
    return pl.pallas_call(
        functools.partial(finish_body, z),
        out_shape=(shape,) * z.prow,
        in_specs=[smem, smem] + [vmem] * (len(arrays) + 1),
        out_specs=(vmem,) * z.prow,
        scratch_shapes=[
            pltpu.VMEM((2, 2 * BS, z.lanes), F32),
            pltpu.VMEM((2, 2 * BS, z.lanes), F32),
            pltpu.VMEM((2 * BS, 2 * BS), F32),
            pltpu.VMEM((2, 2, BS, z.lanes), F32),
            pltpu.VMEM((2 * BS, 4 * BS), F32),
        ],
        compiler_params=pltpu.CompilerParams(vmem_limit_bytes=VMEM_BYTES),
        name="finish_levels",
    )(plan, place, *arrays, corners)


def spread_body(z, plan, place, *refs):
    n = z.prow
    parts, small = refs[:n], refs[n]
    panels, diagonals = refs[n + 1 :]
    p, j = place[3], place[5]
    s = p // (n // 2)
    for cb in range(z.col_blocks):
        span = slice(cb * BS, (cb + 1) * BS)
        at = plan[z.at_place + s * z.col_blocks + cb]
        owner = jnp.where(at < 0, -1, (jnp.maximum(at, 0) // z.slot) ^ p)
        lane = pl.ds(pl.multiple_of((jnp.maximum(at, 0) % z.slot) * BS, BS), BS)

        @pl.when(at < 0)
        def _():
            panels[:, :, span] = jnp.zeros((2, z.piece, BS), F32)

        for d in range(n):
            @pl.when(owner == d)
            def _(d=d):
                panels[:, :, span] = parts[d][:, :, lane]

    @pl.when(j == z.pcol - 1)
    def _():
        panels[1, :, (z.col_blocks - 2) * BS :] = -small[1]

    diagonals[0] = small[0, :, :BS]
    diagonals[1] = small[0, :, BS:]


def spread(z, plan, place, parts, small):
    smem = pl.BlockSpec(memory_space=pltpu.SMEM)
    vmem = pl.BlockSpec(memory_space=pltpu.VMEM)
    return pl.pallas_call(
        functools.partial(spread_body, z),
        out_shape=(
            jax.ShapeDtypeStruct((2, z.piece, z.col_blocks * BS), F32),
            jax.ShapeDtypeStruct((2, z.piece, BS), F32),
        ),
        in_specs=[smem, smem] + [vmem] * (z.prow + 1),
        out_specs=(vmem, vmem),
        compiler_params=pltpu.CompilerParams(vmem_limit_bytes=VMEM_BYTES),
        name="spread_panels",
    )(plan, place, *parts, small)


def whole_run(z, window, pattern, lists, thin_factor, corners, p, j):
    ids = jnp.stack([p, j])
    plan, own = make_plan(z, ids, lists, thin_factor)
    plane, core = j // 2, j % 2
    near = plane // (z.planes // 2)
    first = jnp.logical_and(p == 0, j == 0).astype(jnp.int32)
    place_near = jnp.stack([near, plane, core, p, first, j])
    place_far = jnp.stack([1 - near, plane, core, p, first, j])

    def twin(array, least, most):
        pairs = [(k, k ^ 1) for k in range(z.pcol) if least <= k // 2 <= most]
        return lax.ppermute(array, "pcol", pairs)

    last = z.planes - 1
    streams = {0: (own, twin(own, 0, last))}
    below, above = own, own
    for d in range(1, z.planes):
        below = lax.ppermute(below, "pcol", [(k, k + 2) for k in range(z.pcol - 2) if k // 2 >= d - 1])
        above = lax.ppermute(above, "pcol", [(k, k - 2) for k in range(2, z.pcol) if k // 2 <= last - d + 1])
        streams[-d] = (below, twin(below, d, last))
        streams[d] = (above, twin(above, 0, last - d))

    packed_near = pack_window(z, plan, pattern, place_near, window)
    packed_far = pack_window(z, plan, pattern, place_far, window)
    per = z.planes // 2

    def exchange(arrays):
        return [arrays[0]] + [
            lax.ppermute(arrays[d], "prow", [(k, k ^ d) for k in range(z.prow)]) for d in range(1, z.prow)
        ]

    def from_root(arrays):
        result = [arrays[0]]
        for d in range(1, z.prow):
            pairs = []
            for k in range(z.pcol):
                root = k * z.prow // z.pcol
                pairs.append((root * z.pcol + k, (root ^ d) * z.pcol + k))
            result.append(lax.ppermute(arrays[d], ("prow", "pcol"), pairs))
        return result

    def from_end(array):
        end = z.prow - 1
        return [array] + [lax.ppermute(array, "prow", [(end, end ^ d)]) for d in range(1, z.prow)]

    sums, seats, tail = product(z, range(per), plan, place_near, streams, packed_near)
    near_sum, near_seat, near_tail = exchange(sums), from_root(seats), from_end(tail)
    sums, seats, tail = product(z, range(1, z.planes), plan, place_far, streams, packed_far)
    far_sum, far_seat, far_tail = exchange(sums), from_root(seats), from_end(tail)
    pieces = finish(
        z, plan, place_near, near_sum + far_sum + near_seat + far_seat + near_tail + far_tail, corners
    )
    parts = exchange(pieces)
    small = functools.reduce(lambda a, b: a + b, [part[:, :, z.lanes :] for part in parts])
    small = lax.psum(small, "pcol")
    return spread(z, plan, place_near, parts, small)


def up_to(value, step):
    return -(-value // step) * step


def local(window, pattern, row_lists, factor, diag_inverse):
    p, j = lax.axis_index("prow"), lax.axis_index("pcol")
    prow, pcol = lax.axis_size("prow"), lax.axis_size("pcol")
    rows, cols = window.shape
    row_blocks, col_blocks = rows // BS, cols // BS
    thin_factor = jnp.swapaxes(factor, 1, 2)
    lists = row_lists.reshape(-1)
    pattern = pattern.reshape(-1)
    capacities = []
    for row_cap, col_cap in (
        (row_blocks // 2, 3 * col_blocks // 5),
        (3 * row_blocks // 5, 4 * col_blocks // 5),
        (row_blocks, col_blocks),
    ):
        capacities.append((row_cap, up_to(col_cap, prow)))
    held = row_lists[0]
    row_need = jnp.max(jnp.sum((held // row_blocks)[:, :, None] == jnp.arange(prow), axis=1))
    col_need = jnp.max(jnp.sum((held // col_blocks)[:, :, None] == jnp.arange(pcol), axis=1))
    tier = sum(
        jnp.logical_or(row_need > row_cap, col_need > col_cap).astype(jnp.int32)
        for row_cap, col_cap in capacities[:-1]
    )
    branches = []
    for row_cap, col_cap in capacities:
        z = Sizes(rows, cols, factor.shape[2], prow, pcol, row_lists.shape[2], row_cap, col_cap)
        branches.append(functools.partial(whole_run, z))
    panels, diagonals = lax.switch(
        tier, branches, window, pattern, lists, thin_factor, diag_inverse, p, j
    )
    return jnp.swapaxes(panels, 1, 2), jnp.swapaxes(diagonals, 1, 2)


def solution(mesh):
    in_specs = (P("prow", "pcol"), P("prow", "pcol"), P(), P(None, "prow", "pcol"), P())
    out_specs = (P(None, "pcol", "prow"), P(None, None, "prow"))
    return jax.shard_map(local, mesh=mesh, in_specs=in_specs, out_specs=out_specs, check_vma=False)
```

```python
import functools

import jax
import jax.numpy as jnp
from jax import lax
from jax.experimental import pallas as pl
from jax.experimental.pallas import tpu as pltpu
from jax.sharding import PartitionSpec as P

BS = 128
DEPTH = 4
RING = 3
VMEM_BYTES = 60 * 1024 * 1024

F32 = jnp.float32
BF16 = jnp.bfloat16
exact_mode = lax.Precision.HIGHEST


def up_to(value, step):
    return (value + step - 1) // step * step


class Sizes:
    def __init__(self, rows, cols, thin, prow, pcol, listed, row_cap, col_cap):
        self.prow, self.pcol, self.planes = prow, pcol, pcol // 2
        self.share = pcol // prow
        self.thin, self.listed = thin, listed
        self.rows = rows
        self.row_blocks, self.col_blocks = rows // BS, cols // BS
        self.row_cap, self.col_cap = row_cap, col_cap
        self.deep = up_to(row_cap, DEPTH)
        self.wide = (row_cap + 1) * BS
        self.slot = col_cap // prow
        self.lanes = self.slot * BS
        self.piece = 2 * BS // prow
        self.half = pcol // 2
        self.row_room = up_to(self.row_blocks, DEPTH) + 1
        self.col_room = up_to(self.col_blocks, prow) + 1
        at = 0
        for name, extent in (
            ("at_rows", 2 * self.row_room),
            ("at_cols", 2 * self.col_room),
            ("at_second", 2 * self.col_room),
            ("at_place", 2 * self.col_blocks),
            ("at_pick", self.share * self.col_room),
            ("at_count", 5),
            ("at_tier", 1),
        ):
            setattr(self, name, at)
            at += extent
        self.plan = at


def plan_body(z, capacities, row_caps, ids, lists, thin_ref, plan, *refs):
    owns, (member, full, sem) = refs[: len(row_caps)], refs[len(row_caps) :]
    p, j = ids[0], ids[1]
    mine = 2 * j // z.pcol

    def clear(k, c):
        member[k] = 0
        return c

    lax.fori_loop(0, z.row_blocks * z.prow, clear, 0, unroll=8)

    def blank(k, c):
        plan[k] = 0
        return c

    lax.fori_loop(0, z.at_place, blank, 0, unroll=8)

    def wipe(k, c):
        plan[z.at_place + k] = -1
        return c

    lax.fori_loop(0, z.at_count - z.at_place, wipe, 0, unroll=8)
    for s in range(2):
        def mark(k, c, s=s):
            b = lists[s * z.listed + k]
            member[b] = member[b] | (5 << s)
            return c

        lax.fori_loop(0, z.listed - 2, mark, 0, unroll=8)
        for k in range(z.listed - 2, z.listed):
            b = lists[s * z.listed + k]
            member[b] = member[b] | (1 << s)

    def take_row(r, counts):
        v = member[p * z.row_blocks + r]
        for s in range(2):
            plan[z.at_rows + s * z.row_room + counts[s]] = r
        return tuple(counts[s] + ((v >> s) & 1) for s in range(2))

    row_counts = lax.fori_loop(0, z.row_blocks, take_row, (0, 0), unroll=4)

    def in_order(section, put):
        def take_both(cb, count):
            v = member[section * z.col_blocks + cb]

            @pl.when((v & 3) == 3)
            def _():
                for s in range(2):
                    put(s, count, cb, v)

            return count + ((v & 3) == 3).astype(jnp.int32)

        common = lax.fori_loop(0, z.col_blocks, take_both, 0, unroll=2)

        def take_one(cb, counts):
            v = member[section * z.col_blocks + cb]
            result = []
            for s in range(2):
                single = (v & 3) == (1 << s)

                @pl.when(single)
                def _(s=s):
                    put(s, counts[s], cb, v)

                result.append(counts[s] + single.astype(jnp.int32))
            return tuple(result)

        return lax.fori_loop(0, z.col_blocks, take_one, (common, common), unroll=2) + (common,)

    def put_col(s, t, cb, v):
        plan[z.at_cols + s * z.col_room + t] = cb
        plan[z.at_second + s * z.col_room + t] = (v >> (2 + s)) & 1
        plan[z.at_place + s * z.col_blocks + cb] = t

    for k, value in enumerate(row_counts + in_order(j, put_col)):
        plan[z.at_count + k] = value
    for r in range(z.share):
        def put_pick(s, t, cb, v, r=r):
            @pl.when(s == mine)
            def _():
                plan[z.at_pick + r * z.col_room + t] = 2 * (r * z.col_blocks + cb) + ((v >> (2 + s)) & 1)

        in_order(p * z.share + r, put_pick)

    most_rows, most_cols = 0, 0
    for q in range(z.prow):
        in_row = 0
        for r in range(z.share):
            section = q * z.share + r

            def tally(cb, c, section=section):
                v = member[section * z.col_blocks + cb]
                return c + (v & 1) + ((v & 2) << 15)

            in_col = lax.fori_loop(0, z.col_blocks, tally, 0, unroll=True)
            in_row = in_row + in_col
            most_cols = jnp.maximum(most_cols, jnp.maximum(in_col & 0xFFFF, in_col >> 16))
        most_rows = jnp.maximum(most_rows, jnp.maximum(in_row & 0xFFFF, in_row >> 16))
    tier = 0
    for row_cap, col_cap in capacities[:-1]:
        tier = tier + jnp.logical_or(most_rows > row_cap, most_cols > col_cap).astype(jnp.int32)
    plan[z.at_tier] = tier

    held = plan[z.at_count + mine]

    def pack(k, c):
        r = plan[z.at_rows + mine * z.row_room + k]
        second = (member[p * z.row_blocks + r] >> (2 + mine)) & 1
        source = pl.ds(pl.multiple_of(r * BS, BS), BS)
        target = pl.ds(pl.multiple_of(k * BS, BS), BS)
        full[0, :, target] = thin_ref[0, :, source]
        full[1, :, target] = jnp.where(second == 1, thin_ref[1, :, source], 0.0)
        return c

    lax.fori_loop(0, held, pack, 0)

    def pad(k, c):
        full[:, :, pl.ds(pl.multiple_of(k * BS, BS), BS)] = jnp.zeros((2, z.thin, BS), F32)
        return c

    lax.fori_loop(held, z.row_blocks, pad, 0)
    for row_cap, own in zip(row_caps, owns):
        wanted = functools.reduce(
            jnp.logical_or, [tier == k for k, pair in enumerate(capacities) if pair[0] == row_cap]
        )

        @pl.when(wanted)
        def _(row_cap=row_cap, own=own):
            for q in range(2):
                full[q, :, row_cap * BS : (row_cap + 1) * BS] = thin_ref[
                    1, :, z.rows - (2 - q) * BS : z.rows - (1 - q) * BS
                ]
            copy = pltpu.make_async_copy(full.at[:, :, : (row_cap + 1) * BS], own, sem)
            copy.start()
            copy.wait()


def make_plan(z, capacities, ids, lists, thin_factor):
    row_caps = sorted({pair[0] for pair in capacities})
    smem = pl.BlockSpec(memory_space=pltpu.SMEM)
    vmem = pl.BlockSpec(memory_space=pltpu.VMEM)
    anywhere = pl.BlockSpec(memory_space=pl.ANY)
    plan, *owns = pl.pallas_call(
        functools.partial(plan_body, z, capacities, row_caps),
        out_shape=(jax.ShapeDtypeStruct((z.plan,), jnp.int32),)
        + tuple(jax.ShapeDtypeStruct((2, z.thin, (cap + 1) * BS), F32) for cap in row_caps),
        in_specs=[smem, smem, vmem],
        out_specs=(smem,) + (anywhere,) * len(row_caps),
        scratch_shapes=[
            pltpu.SMEM((z.row_blocks * z.prow,), jnp.int32),
            pltpu.VMEM((2, z.thin, (z.row_blocks + 1) * BS), F32),
            pltpu.SemaphoreType.DMA,
        ],
        compiler_params=pltpu.CompilerParams(vmem_limit_bytes=VMEM_BYTES),
        name="plan_rows",
    )(ids, lists, thin_factor)
    return plan, dict(zip(row_caps, owns))


def pick_body(z, plan, place, thin_ref, *outs):
    p = place[3]
    for d in range(z.prow):
        for r in range(z.share):
            for t in range(z.slot):
                v = plan[z.at_pick + r * z.col_room + (p ^ d) * z.slot + t]
                span = slice(t * BS, (t + 1) * BS)
                source = pl.ds(pl.multiple_of((jnp.maximum(v, 0) >> 1) * BS, BS), BS)
                outs[d][r, 0, :, span] = jnp.where(v >= 0, thin_ref[0, :, source], 0.0)
                outs[d][r, 1, :, span] = jnp.where(
                    jnp.logical_and(v >= 0, (v & 1) == 1), thin_ref[1, :, source], 0.0
                )


def pick(z, plan, place, thin_factor):
    smem = pl.BlockSpec(memory_space=pltpu.SMEM)
    vmem = pl.BlockSpec(memory_space=pltpu.VMEM)
    return pl.pallas_call(
        functools.partial(pick_body, z),
        out_shape=(jax.ShapeDtypeStruct((z.share, 2, z.thin, z.lanes), F32),) * z.prow,
        in_specs=[smem, smem, vmem],
        out_specs=(vmem,) * z.prow,
        compiler_params=pltpu.CompilerParams(vmem_limit_bytes=VMEM_BYTES),
        name="pick_blocks",
    )(plan, place, thin_factor)


def route_body(z, place, *refs):
    sources, outs, sems = refs[: z.prow], refs[z.prow : -1], refs[-1]
    plane, core, p = place[1], place[2], place[3]
    for step in range(z.planes):
        for e in range(2):
            k = 2 * step + e
            for d in range(z.prow):
                @pl.when((p ^ plane ^ step) == d)
                def _(k=k, d=d, e=e):
                    pltpu.make_async_copy(sources[d].at[core ^ e], outs[k], sems.at[k]).start()
    for k, out in enumerate(outs):
        pltpu.make_async_copy(sources[0].at[0], out, sems.at[k]).wait()


def route(z, place, sources):
    smem = pl.BlockSpec(memory_space=pltpu.SMEM)
    anywhere = pl.BlockSpec(memory_space=pl.ANY)
    return pl.pallas_call(
        functools.partial(route_body, z),
        out_shape=(jax.ShapeDtypeStruct((2, z.thin, z.lanes), F32),) * z.pcol,
        in_specs=[smem] + [anywhere] * z.prow,
        out_specs=(anywhere,) * z.pcol,
        scratch_shapes=[pltpu.SemaphoreType.DMA((z.pcol,))],
        compiler_params=pltpu.CompilerParams(vmem_limit_bytes=VMEM_BYTES),
        name="route_blocks",
    )(place, *sources)


def pack_body(z, plan, pattern, place, strip, high, low):
    k = pl.program_id(0)
    s = place[0]
    rows, cols = plan[z.at_count + s], plan[z.at_count + 2 + s]

    @pl.when(k < up_to(rows, DEPTH))
    def _():
        r = plan[z.at_rows + s * z.row_room + k]

        def fill(t, c):
            cb = plan[z.at_cols + s * z.col_room + t]
            keep = jnp.logical_and(k < rows, pattern[r * z.col_blocks + cb] > 0)
            block = jnp.where(keep, strip[:, pl.ds(pl.multiple_of(cb * BS, BS), BS)], 0.0)
            span = pl.ds(pl.multiple_of(t * BS, BS), BS)
            top = block.astype(BF16)
            high[:, span] = top
            low[:, span] = (block - top.astype(F32)).astype(BF16)
            return c

        lax.fori_loop(0, cols, fill, 0)

        def pad(t, c):
            span = pl.ds(pl.multiple_of(t * BS, BS), BS)
            high[:, span] = jnp.zeros((BS, BS), BF16)
            low[:, span] = jnp.zeros((BS, BS), BF16)
            return c

        lax.fori_loop(cols, up_to(cols, z.slot), pad, 0)


def pack_window(z, plan, pattern, place, window):
    def strip_at(k, plan, pattern, place):
        s = place[0]
        last = jnp.maximum(plan[z.at_count + s] - 1, 0)
        return plan[z.at_rows + s * z.row_room + jnp.minimum(k, last)], 0

    def kept_at(k, plan, pattern, place):
        last = jnp.maximum(up_to(plan[z.at_count + place[0]], DEPTH) - 1, 0)
        return jnp.minimum(k, last), 0

    kept = pl.BlockSpec((BS, z.col_cap * BS), kept_at)
    shape = jax.ShapeDtypeStruct((z.deep * BS, z.col_cap * BS), BF16)
    return pl.pallas_call(
        functools.partial(pack_body, z),
        out_shape=(shape, shape),
        grid_spec=pltpu.PrefetchScalarGridSpec(
            num_scalar_prefetch=3,
            grid=(z.deep,),
            in_specs=[pl.BlockSpec((BS, z.col_blocks * BS), strip_at)],
            out_specs=(kept, kept),
        ),
        compiler_params=pltpu.CompilerParams(vmem_limit_bytes=VMEM_BYTES),
        cost_estimate=pl.CostEstimate(
            flops=0, transcendentals=0, bytes_accessed=z.deep * BS * z.col_blocks * BS * 6
        ),
        name="pack_window",
    )(plan, pattern, place, window)


def product_body(z, reach, plan, place, *refs):
    names = [0] if 0 in reach else []
    for d in reach:
        if d > 0:
            names += [-d, d]
    count = 2 * len(names)
    sources = {step: (refs[2 * k], refs[2 * k + 1]) for k, step in enumerate(names)}
    packed = refs[count : count + 2]
    sums = refs[count + 2 : count + 2 + z.prow]
    tail, raw, top, rest, total, ring, sems, ring_sems = refs[count + 2 + z.prow :]
    s, plane, core, p = place[0], place[1], place[2], place[3]
    per = z.planes // 2
    for qi in range(per):
        away = s * per + qi - plane
        for c in range(2):
            slot = qi * 2 + c
            for step, pair in sources.items():
                for k in range(2):
                    @pl.when(jnp.logical_and(away == step, (c == core) == (k == 0)))
                    def _(pair=pair, k=k, slot=slot):
                        pltpu.make_async_copy(pair[k], raw.at[slot], sems.at[slot]).start()

    cols = plan[z.at_count + 2 + s]
    depth = (plan[z.at_count + s] + DEPTH - 1) // DEPTH
    subsets = jnp.where(depth > 0, (cols + z.slot - 1) // z.slot, 0)
    jobs = subsets * depth

    def fetch(i, k, at):
        rows = pl.ds(pl.multiple_of(k * DEPTH * BS, DEPTH * BS), DEPTH * BS)
        lanes = pl.ds(pl.multiple_of(i * z.lanes, BS), z.lanes)
        return [
            pltpu.make_async_copy(packed[h].at[rows, lanes], ring.at[at, h], ring_sems.at[at, h])
            for h in range(2)
        ]

    def request(n, i, k, at):
        @pl.when(n < jobs)
        def _():
            for copy in fetch(i, k, at):
                copy.start()

        turn = k + 1 == depth
        return jnp.where(turn, i + 1, i), jnp.where(turn, 0, k + 1), jnp.where(at + 1 == RING, 0, at + 1)

    ahead = (jnp.int32(0), jnp.int32(0), jnp.int32(0))
    for n in range(RING - 1):
        ahead = request(n, *ahead)

    any_source = next(iter(sources.values()))[0]
    for slot in range(z.half):
        pltpu.make_async_copy(any_source, raw.at[slot], sems.at[slot]).wait()
        for level in range(2):
            rows = slice(level * BS + slot * z.thin, level * BS + (slot + 1) * z.thin)
            value = raw[slot, level, :, : z.row_cap * BS]
            head = value.astype(BF16)
            top[rows, : z.row_cap * BS] = head
            rest[rows, : z.row_cap * BS] = (value - head.astype(F32)).astype(BF16)
            if z.deep > z.row_cap:
                blank = jnp.zeros((z.thin, (z.deep - z.row_cap) * BS), BF16)
                top[rows, z.row_cap * BS :] = blank
                rest[rows, z.row_cap * BS :] = blank
            tail[slot * z.thin : (slot + 1) * z.thin, level * BS : (level + 1) * BS] = jnp.where(
                p == z.prow - 1, raw[slot, level, :, z.row_cap * BS :], 0.0
            )
    for d in range(z.prow):
        @pl.when((p ^ d) >= subsets)
        def _(d=d):
            sums[d][...] = jnp.zeros_like(sums[d])

    def one_subset(i, carry):
        def one_depth(k, carry):
            n, at, ahead = carry
            ahead = request(n + RING - 1, *ahead)
            for copy in fetch(i, k, at):
                copy.wait()
            span = pl.ds(pl.multiple_of(k * DEPTH * BS, DEPTH * BS), DEPTH * BS)
            x_top, x_rest = top[:, span], rest[:, span]
            part = (
                jnp.dot(x_top, ring[at, 1], preferred_element_type=F32)
                + jnp.dot(x_rest, ring[at, 0], preferred_element_type=F32)
                + jnp.dot(x_top, ring[at, 0], preferred_element_type=F32)
            )

            @pl.when(k == 0)
            def _():
                total[...] = part

            @pl.when(k > 0)
            def _():
                total[...] += part

            return n + 1, jnp.where(at + 1 == RING, 0, at + 1), ahead

        carry = lax.fori_loop(0, depth, one_depth, carry)
        for d in range(z.prow):
            @pl.when((i ^ p) == d)
            def _(d=d):
                sums[d][...] = total[...]

        return carry

    lax.fori_loop(0, subsets, one_subset, (jnp.int32(0), jnp.int32(0), ahead))


def product(z, reach, plan, place, streams, packed):
    arrays = []
    if 0 in reach:
        arrays += list(streams[0])
    for d in reach:
        if d > 0:
            arrays += list(streams[-d]) + list(streams[d])
    smem = pl.BlockSpec(memory_space=pltpu.SMEM)
    vmem = pl.BlockSpec(memory_space=pltpu.VMEM)
    anywhere = pl.BlockSpec(memory_space=pl.ANY)
    shape = jax.ShapeDtypeStruct((2 * BS, z.lanes), F32)
    out = pl.pallas_call(
        functools.partial(product_body, z, reach),
        out_shape=(shape,) * z.prow + (jax.ShapeDtypeStruct((BS, 2 * BS), F32),),
        in_specs=[smem, smem] + [anywhere] * (len(arrays) + 2),
        out_specs=(vmem,) * (z.prow + 1),
        scratch_shapes=[
            pltpu.VMEM((z.half, 2, z.thin, z.wide), F32),
            pltpu.VMEM((2 * BS, z.deep * BS), BF16),
            pltpu.VMEM((2 * BS, z.deep * BS), BF16),
            pltpu.VMEM((2 * BS, z.lanes), F32),
            pltpu.VMEM((RING, 2, DEPTH * BS, z.lanes), BF16),
            pltpu.SemaphoreType.DMA((z.half,)),
            pltpu.SemaphoreType.DMA((RING, 2)),
        ],
        compiler_params=pltpu.CompilerParams(vmem_limit_bytes=VMEM_BYTES),
        cost_estimate=pl.CostEstimate(
            flops=6 * 2 * BS * z.row_cap * BS * z.col_cap * BS,
            transcendentals=0,
            bytes_accessed=z.deep * BS * z.col_cap * BS * 4,
        ),
        name="window_product",
    )(plan, place, *arrays, *packed)
    return list(out[: z.prow]), out[z.prow]


def plain(left, right):
    return jnp.dot(left, right, precision=exact_mode, preferred_element_type=F32)


def across(left, right):
    return lax.dot_general(
        left, right, (((1,), (1,)), ((), ())), precision=exact_mode, preferred_element_type=F32
    )


def finish_body(z, plan, place, *refs):
    n = z.prow
    near_sum, far_sum = refs[:n], refs[n : 2 * n]
    near_tail, far_tail = refs[2 * n : 3 * n], refs[3 * n : 4 * n]
    shards = refs[4 * n : 4 * n + z.pcol]
    corners = refs[4 * n + z.pcol]
    outs = refs[4 * n + z.pcol + 1 : 6 * n + z.pcol + 1]
    image, live, tails, done, small = refs[6 * n + z.pcol + 1 :]
    near, plane, core, p, first = place[0], place[1], place[2], place[3], place[4]
    for s, sums, ends in ((near, near_sum, near_tail), (1 - near, far_sum, far_tail)):
        image[s] = functools.reduce(lambda a, b: a + b, [r[...] for r in sums])
        tails[pl.ds(pl.multiple_of(s * BS, BS), BS), :] = functools.reduce(
            lambda a, b: a + b, [r[...] for r in ends]
        )
    for k, shard in enumerate(shards):
        owner = 2 * (plane ^ (k // 2)) + (core ^ (k % 2))
        s, slot = owner // z.half, owner % z.half
        for level in range(2):
            live[s, pl.ds(pl.multiple_of(level * BS + slot * z.thin, z.thin), z.thin), :] = shard[level]
    lane = lax.broadcasted_iota(jnp.int32, (1, z.lanes), 1) // BS + p * z.slot
    shared = lane < plan[z.at_count + 4]
    for s in range(2):
        other = 1 - s
        keep = jnp.zeros((1, z.lanes), F32)
        for t in range(z.slot):
            flag = plan[z.at_second + s * z.col_room + p * z.slot + t].astype(F32)
            keep = jnp.where(lane == p * z.slot + t, flag, keep)
        own_first = image[s, :BS, :]
        other_first = jnp.where(shared, image[other, :BS, :], 0.0)
        tail = tails[s * BS : (s + 1) * BS, :]
        second = (
            image[s, BS:, :]
            - plain(tail[:, s * BS : (s + 1) * BS], own_first)
            - plain(tail[:, other * BS : (other + 1) * BS], other_first)
        )
        done[s, 0] = -own_first
        done[s, 1] = -(second * keep)
        live_second = live[s, BS:, :]
        started = jnp.where(first == 1, 1.0, 0.0)
        gram = across(own_first, live[s, :BS, :]) + started * corners[0, :, s * BS : (s + 1) * BS].T
        small[s * BS : (s + 1) * BS, :BS] = gram
        small[s * BS : (s + 1) * BS, BS : 2 * BS] = (
            across(second, live_second) + started * corners[1, :, s * BS : (s + 1) * BS].T
        )
        block = slice(2 * BS + s * BS, 2 * BS + (s + 1) * BS)
        crossed = plain(tails[:, s * BS : (s + 1) * BS], gram)
        small[s * BS : (s + 1) * BS, block] = crossed[s * BS : (s + 1) * BS] - across(live_second, own_first)
        small[other * BS : (other + 1) * BS, block] = crossed[other * BS : (other + 1) * BS] - across(
            jnp.where(shared, live[other, BS:, :], 0.0), own_first
        )
    for s in range(2):
        rows = slice(s * BS, (s + 1) * BS)
        small[rows, BS : 2 * BS] += across(small[rows, 2 * BS :], tails[rows, :])
    per = n // 2
    for d in range(n):
        q = p ^ d
        s, h = q // per, q % per
        for level in range(2):
            outs[d][level] = done[s, level, pl.ds(pl.multiple_of(h * z.piece, z.piece), z.piece), :]
            outs[n + d][level] = small[
                pl.ds(pl.multiple_of(q * z.piece, z.piece), z.piece), level * 2 * BS : (level + 1) * 2 * BS
            ]


def finish(z, plan, place, arrays, corners):
    smem = pl.BlockSpec(memory_space=pltpu.SMEM)
    vmem = pl.BlockSpec(memory_space=pltpu.VMEM)
    out = pl.pallas_call(
        functools.partial(finish_body, z),
        out_shape=(jax.ShapeDtypeStruct((2, z.piece, z.lanes), F32),) * z.prow
        + (jax.ShapeDtypeStruct((2, z.piece, 2 * BS), F32),) * z.prow,
        in_specs=[smem, smem] + [vmem] * (len(arrays) + 1),
        out_specs=(vmem,) * (2 * z.prow),
        scratch_shapes=[
            pltpu.VMEM((2, 2 * BS, z.lanes), F32),
            pltpu.VMEM((2, 2 * BS, z.lanes), F32),
            pltpu.VMEM((2 * BS, 2 * BS), F32),
            pltpu.VMEM((2, 2, BS, z.lanes), F32),
            pltpu.VMEM((2 * BS, 4 * BS), F32),
        ],
        compiler_params=pltpu.CompilerParams(vmem_limit_bytes=VMEM_BYTES),
        name="finish_levels",
    )(plan, place, *arrays, corners)
    return out[: z.prow], out[z.prow :]


def spread_body(z, plan, place, *refs):
    n = z.prow
    parts, small = refs[:n], refs[n]
    panels, diagonals = refs[n + 1 :]
    p, j = place[3], place[5]
    s = p // (n // 2)
    for cb in range(z.col_blocks):
        span = slice(cb * BS, (cb + 1) * BS)
        at = plan[z.at_place + s * z.col_blocks + cb]
        owner = jnp.where(at < 0, -1, (jnp.maximum(at, 0) // z.slot) ^ p)
        lane = pl.ds(pl.multiple_of((jnp.maximum(at, 0) % z.slot) * BS, BS), BS)

        @pl.when(at < 0)
        def _():
            panels[:, :, span] = jnp.zeros((2, z.piece, BS), F32)

        for d in range(n):
            @pl.when(owner == d)
            def _(d=d):
                panels[:, :, span] = parts[d][:, :, lane]

    @pl.when(j == z.pcol - 1)
    def _():
        panels[1, :, (z.col_blocks - 2) * BS :] = -small[1]

    diagonals[0] = small[0, :, :BS]
    diagonals[1] = small[0, :, BS:]


def spread(z, plan, place, parts, small):
    smem = pl.BlockSpec(memory_space=pltpu.SMEM)
    vmem = pl.BlockSpec(memory_space=pltpu.VMEM)
    return pl.pallas_call(
        functools.partial(spread_body, z),
        out_shape=(
            jax.ShapeDtypeStruct((2, z.piece, z.col_blocks * BS), F32),
            jax.ShapeDtypeStruct((2, z.piece, BS), F32),
        ),
        in_specs=[smem, smem] + [vmem] * (z.prow + 1),
        out_specs=(vmem, vmem),
        compiler_params=pltpu.CompilerParams(vmem_limit_bytes=VMEM_BYTES),
        name="spread_panels",
    )(plan, place, *parts, small)


def whole_run(z, window, pattern, plan, own, thin_factor, corners, p, j):
    plane, core = j // 2, j % 2
    near = plane // (z.planes // 2)
    first = jnp.logical_and(p == 0, j == 0).astype(jnp.int32)
    place_near = jnp.stack([near, plane, core, p, first, j])
    place_far = jnp.stack([1 - near, plane, core, p, first, j])

    def twin(array, least, most):
        pairs = [(k, k ^ 1) for k in range(z.pcol) if least <= k // 2 <= most]
        return lax.ppermute(array, "pcol", pairs)

    def exchange(arrays):
        return [arrays[0]] + [
            lax.ppermute(arrays[d], "prow", [(k, k ^ d) for k in range(z.prow)]) for d in range(1, z.prow)
        ]

    def from_end(array):
        end = z.prow - 1
        return [array] + [lax.ppermute(array, "prow", [(end, end ^ d)]) for d in range(1, z.prow)]

    last = z.planes - 1
    per = z.planes // 2
    packed = {}
    streams = {0: (own, twin(own, 0, last))}
    below, above = own, own
    for d in range(1, z.planes):
        below = lax.ppermute(below, "pcol", [(k, k + 2) for k in range(z.pcol - 2) if k // 2 >= d - 1])
        above = lax.ppermute(above, "pcol", [(k, k - 2) for k in range(2, z.pcol) if k // 2 <= last - d + 1])
        if d == 1:
            picked = exchange(pick(z, plan, place_near, thin_factor))
            packed[0] = pack_window(z, plan, pattern, place_near, window)
            below, above, packed[0] = lax.optimization_barrier((below, above, packed[0]))
        if d == 2:
            packed[1] = pack_window(z, plan, pattern, place_far, window)
            below, above, packed[1] = lax.optimization_barrier((below, above, packed[1]))
        if d == last:
            near_sum, near_tail = product(z, range(per), plan, place_near, streams, packed[0])
            below, above, near_sum = lax.optimization_barrier((below, above, near_sum))
        streams[-d] = (below, twin(below, d, last))
        streams[d] = (above, twin(above, 0, last - d))

    near_sum, near_tail = exchange(near_sum), from_end(near_tail)
    far_sum, far_tail = product(z, range(1, z.planes), plan, place_far, streams, packed[1])
    routed = route(z, place_near, picked)
    far_sum, routed = lax.optimization_barrier((far_sum, list(routed)))
    far_sum, far_tail = exchange(far_sum), from_end(far_tail)
    shards = [routed[0]] + [
        lax.ppermute(routed[k], "pcol", [(c, c ^ k) for c in range(z.pcol)]) for k in range(1, z.pcol)
    ]
    parts, small = finish(z, plan, place_near, near_sum + far_sum + near_tail + far_tail + shards, corners)
    small = functools.reduce(lambda a, b: a + b, exchange(small))
    step = 1
    while step < z.pcol:
        small = small + lax.ppermute(small, "pcol", [(k, k ^ step) for k in range(z.pcol)])
        step *= 2
    return spread(z, plan, place_near, exchange(parts), small)


def local(window, pattern, row_lists, factor, diag_inverse):
    p, j = lax.axis_index("prow"), lax.axis_index("pcol")
    prow, pcol = lax.axis_size("prow"), lax.axis_size("pcol")
    rows, cols = window.shape
    row_blocks, col_blocks = rows // BS, cols // BS
    thin_factor = jnp.swapaxes(factor, 1, 2)
    capacities = [
        (row_cap, up_to(col_cap, prow))
        for row_cap, col_cap in (
            (row_blocks // 2, 3 * col_blocks // 5),
            (3 * row_blocks // 5, 3 * col_blocks // 5),
            (3 * row_blocks // 5, 4 * col_blocks // 5),
            (row_blocks, col_blocks),
        )
    ]
    sizes = [
        Sizes(rows, cols, factor.shape[2], prow, pcol, row_lists.shape[2], row_cap, col_cap)
        for row_cap, col_cap in capacities
    ]
    plan, owns = make_plan(sizes[-1], capacities, jnp.stack([p, j]), row_lists.reshape(-1), thin_factor)

    def branch(z, pattern, *rest):
        return whole_run(z, rest[0], pattern, plan, owns[z.row_cap], thin_factor, diag_inverse, p, j)

    panels, diagonals = lax.switch(
        plan[sizes[-1].at_tier],
        [functools.partial(branch, z) for z in sizes],
        pattern.reshape(-1),
        window,
    )
    return jnp.swapaxes(panels, 1, 2), jnp.swapaxes(diagonals, 1, 2)


def solution(mesh):
    in_specs = (P("prow", "pcol"), P("prow", "pcol"), P(), P(None, "prow", "pcol"), P())
    out_specs = (P(None, "pcol", "prow"), P(None, None, "prow"))
    return jax.shard_map(local, mesh=mesh, in_specs=in_specs, out_specs=out_specs, check_vma=False)
```

```python
import functools

import jax
import jax.numpy as jnp
from jax import lax
from jax.experimental import pallas as pl
from jax.experimental.pallas import tpu as pltpu
from jax.sharding import PartitionSpec as P

BS = 128
DEPTH = 4
RING = 3
VMEM_BYTES = 60 * 1024 * 1024

F32 = jnp.float32
BF16 = jnp.bfloat16
exact_mode = lax.Precision.HIGHEST


def up_to(value, step):
    return (value + step - 1) // step * step


class Sizes:
    def __init__(self, rows, cols, thin, prow, pcol, listed, row_cap, col_cap):
        self.prow, self.pcol, self.planes = prow, pcol, pcol // 2
        self.share = pcol // prow
        self.thin, self.listed = thin, listed
        self.rows = rows
        self.row_blocks, self.col_blocks = rows // BS, cols // BS
        self.row_cap, self.col_cap = row_cap, col_cap
        self.deep = up_to(row_cap, DEPTH)
        self.wide = row_cap * BS
        self.slot = col_cap // prow
        self.lanes = self.slot * BS
        self.long = self.lanes + BS
        self.piece = 2 * BS // prow
        self.half = pcol // 2
        self.row_room = up_to(self.row_blocks, DEPTH) + 1
        self.col_room = up_to(self.col_blocks, prow) + 1
        at = 0
        for name, extent in (
            ("at_rows", 2 * self.row_room),
            ("at_cols", 2 * self.col_room),
            ("at_second", 2 * self.col_room),
            ("at_place", 2 * self.col_blocks),
            ("at_pick", self.share * self.col_room),
            ("at_count", 5),
        ):
            setattr(self, name, at)
            at += extent
        self.plan = at


def plan_body(z, capacities, row_caps, lists, thin_ref, plan, chosen, *refs):
    owns, (member, full, sem) = refs[: len(row_caps)], refs[len(row_caps) :]
    p, j = lax.axis_index("prow"), lax.axis_index("pcol")
    mine = 2 * j // z.pcol

    def clear(k, c):
        member[k] = 0
        return c

    lax.fori_loop(0, z.row_blocks * z.prow, clear, 0, unroll=8)

    def blank(k, c):
        plan[k] = 0
        return c

    lax.fori_loop(0, z.at_place, blank, 0, unroll=8)

    def wipe(k, c):
        plan[z.at_place + k] = -1
        return c

    lax.fori_loop(0, z.at_count - z.at_place, wipe, 0, unroll=8)
    for s in range(2):
        def mark(k, c, s=s):
            b = lists[0, s, k]
            member[b] = member[b] | (5 << s)
            return c

        lax.fori_loop(0, z.listed - 2, mark, 0, unroll=8)
        for k in range(z.listed - 2, z.listed):
            b = lists[0, s, k]
            member[b] = member[b] | (1 << s)

    def take_row(r, counts):
        v = member[p * z.row_blocks + r]
        for s in range(2):
            plan[z.at_rows + s * z.row_room + counts[s]] = r
        return tuple(counts[s] + ((v >> s) & 1) for s in range(2))

    row_counts = lax.fori_loop(0, z.row_blocks, take_row, (0, 0), unroll=4)

    def in_order(section, put):
        def take_both(cb, count):
            v = member[section * z.col_blocks + cb]

            @pl.when((v & 3) == 3)
            def _():
                for s in range(2):
                    put(s, count, cb, v)

            return count + ((v & 3) == 3).astype(jnp.int32)

        common = lax.fori_loop(0, z.col_blocks, take_both, 0, unroll=2)

        def take_one(cb, counts):
            v = member[section * z.col_blocks + cb]
            result = []
            for s in range(2):
                single = (v & 3) == (1 << s)

                @pl.when(single)
                def _(s=s):
                    put(s, counts[s], cb, v)

                result.append(counts[s] + single.astype(jnp.int32))
            return tuple(result)

        return lax.fori_loop(0, z.col_blocks, take_one, (common, common), unroll=2) + (common,)

    def put_col(s, t, cb, v):
        plan[z.at_cols + s * z.col_room + t] = cb
        plan[z.at_second + s * z.col_room + t] = (v >> (2 + s)) & 1
        plan[z.at_place + s * z.col_blocks + cb] = t

    for k, value in enumerate(row_counts + in_order(j, put_col)):
        plan[z.at_count + k] = value
    for r in range(z.share):
        def put_pick(s, t, cb, v, r=r):
            @pl.when(s == mine)
            def _():
                plan[z.at_pick + r * z.col_room + t] = 2 * (r * z.col_blocks + cb) + ((v >> (2 + s)) & 1)

        in_order(p * z.share + r, put_pick)

    most_rows, most_cols = 0, 0
    for q in range(z.prow):
        in_row = 0
        for r in range(z.share):
            section = q * z.share + r

            def tally(cb, c, section=section):
                v = member[section * z.col_blocks + cb]
                return c + (v & 1) + ((v & 2) << 15)

            in_col = lax.fori_loop(0, z.col_blocks, tally, 0, unroll=True)
            in_row = in_row + in_col
            most_cols = jnp.maximum(most_cols, jnp.maximum(in_col & 0xFFFF, in_col >> 16))
        most_rows = jnp.maximum(most_rows, jnp.maximum(in_row & 0xFFFF, in_row >> 16))
    tier = 0
    for row_cap, col_cap in capacities[:-1]:
        tier = tier + jnp.logical_or(most_rows > row_cap, most_cols > col_cap).astype(jnp.int32)
    chosen[0] = tier

    held = plan[z.at_count + mine]

    def pack(k, c):
        r = plan[z.at_rows + mine * z.row_room + k]
        second = (member[p * z.row_blocks + r] >> (2 + mine)) & 1
        source = pl.ds(pl.multiple_of(r * BS, BS), BS)
        target = pl.ds(pl.multiple_of(k * BS, BS), BS)
        full[0, :, target] = thin_ref[0, :, source]
        full[1, :, target] = jnp.where(second == 1, thin_ref[1, :, source], 0.0)
        return c

    lax.fori_loop(0, held, pack, 0)

    def pad(k, c):
        full[:, :, pl.ds(pl.multiple_of(k * BS, BS), BS)] = jnp.zeros((2, z.thin, BS), F32)
        return c

    lax.fori_loop(held, z.row_blocks, pad, 0)
    for row_cap, own in zip(row_caps, owns):
        wanted = functools.reduce(
            jnp.logical_or, [tier == k for k, pair in enumerate(capacities) if pair[0] == row_cap]
        )

        @pl.when(wanted)
        def _(row_cap=row_cap, own=own):
            copy = pltpu.make_async_copy(full.at[:, :, : row_cap * BS], own, sem)
            copy.start()
            copy.wait()


def make_plan(z, capacities, lists, thin_factor):
    row_caps = sorted({pair[0] for pair in capacities})
    smem = pl.BlockSpec(memory_space=pltpu.SMEM)
    vmem = pl.BlockSpec(memory_space=pltpu.VMEM)
    anywhere = pl.BlockSpec(memory_space=pl.ANY)
    plan, chosen, *owns = pl.pallas_call(
        functools.partial(plan_body, z, capacities, row_caps),
        out_shape=(jax.ShapeDtypeStruct((z.plan,), jnp.int32), jax.ShapeDtypeStruct((1,), jnp.int32))
        + tuple(jax.ShapeDtypeStruct((2, z.thin, cap * BS), F32) for cap in row_caps),
        in_specs=[smem, vmem],
        out_specs=(smem, smem) + (anywhere,) * len(row_caps),
        scratch_shapes=[
            pltpu.SMEM((z.row_blocks * z.prow,), jnp.int32),
            pltpu.VMEM((2, z.thin, z.row_blocks * BS), F32),
            pltpu.SemaphoreType.DMA,
        ],
        compiler_params=pltpu.CompilerParams(vmem_limit_bytes=VMEM_BYTES),
        name="plan_rows",
    )(lists, thin_factor)
    return plan, chosen, dict(zip(row_caps, owns))


def supernode(z, far):
    near = lax.axis_index("pcol") // z.half
    return 1 - near if far else near


def pick_body(z, plan, thin_ref, *outs):
    p = lax.axis_index("prow")
    for d in range(z.prow):
        for r in range(z.share):
            for t in range(z.slot):
                v = plan[z.at_pick + r * z.col_room + (p ^ d) * z.slot + t]
                span = slice(t * BS, (t + 1) * BS)
                source = pl.ds(pl.multiple_of((jnp.maximum(v, 0) >> 1) * BS, BS), BS)
                outs[d][r, 0, :, span] = jnp.where(v >= 0, thin_ref[0, :, source], 0.0)
                outs[d][r, 1, :, span] = jnp.where(
                    jnp.logical_and(v >= 0, (v & 1) == 1), thin_ref[1, :, source], 0.0
                )
            for q in range(2):
                outs[d][r, q, :, z.lanes :] = thin_ref[1, :, z.rows - (2 - q) * BS : z.rows - (1 - q) * BS]


def pick(z, plan, thin_factor):
    smem = pl.BlockSpec(memory_space=pltpu.SMEM)
    vmem = pl.BlockSpec(memory_space=pltpu.VMEM)
    return pl.pallas_call(
        functools.partial(pick_body, z),
        out_shape=(jax.ShapeDtypeStruct((z.share, 2, z.thin, z.long), F32),) * z.prow,
        in_specs=[smem, vmem],
        out_specs=(vmem,) * z.prow,
        compiler_params=pltpu.CompilerParams(vmem_limit_bytes=VMEM_BYTES),
        name="pick_blocks",
    )(plan, thin_factor)


def route_body(z, *refs):
    sources, (keep, give) = refs[: z.prow], refs[z.prow :]
    p, j = lax.axis_index("prow"), lax.axis_index("pcol")
    plane, core = j // 2, j % 2
    for step in range(z.planes):
        for d in range(z.prow):
            @pl.when((p ^ plane ^ step) == d)
            def _(step=step, d=d):
                keep[step, :, :, : z.lanes] = sources[d][core, :, :, : z.lanes]
                give[step, :, :, : z.lanes] = sources[d][1 - core, :, :, : z.lanes]

    for d in range(z.prow):
        @pl.when((p ^ d) == z.prow - 1)
        def _(d=d):
            for step in range(z.planes):
                keep[step, :, :, z.lanes :] = sources[d][0, :, :, z.lanes :]
                give[step, :, :, z.lanes :] = sources[d][0, :, :, z.lanes :]


def route(z, sources):
    vmem = pl.BlockSpec(memory_space=pltpu.VMEM)
    return pl.pallas_call(
        functools.partial(route_body, z),
        out_shape=(jax.ShapeDtypeStruct((z.planes, 2, z.thin, z.long), F32),) * 2,
        in_specs=[vmem] * z.prow,
        out_specs=(vmem, vmem),
        compiler_params=pltpu.CompilerParams(vmem_limit_bytes=VMEM_BYTES),
        name="route_blocks",
    )(*sources)


def pack_body(z, far, plan, pattern, window, high, low, blocks, halves, in_sems, out_sems):
    s = supernode(z, far)
    rows, cols = plan[z.at_count + s], plan[z.at_count + 2 + s]
    subsets = (cols + z.slot - 1) // z.slot
    steps = up_to(rows, DEPTH)

    def fetch(k):
        @pl.when(k < rows)
        def _():
            r = plan[z.at_rows + s * z.row_room + k]

            def one(t, c):
                cb = plan[z.at_cols + s * z.col_room + t]
                pltpu.make_async_copy(
                    window.at[pl.ds(pl.multiple_of(r * BS, BS), BS), pl.ds(pl.multiple_of(cb * BS, BS), BS)],
                    blocks.at[k & 3, t],
                    in_sems.at[k & 3],
                ).start()
                return c

            lax.fori_loop(0, cols, one, 0)

    def outgoing(k, i):
        lanes = pl.ds(pl.multiple_of(i * z.lanes, BS), z.lanes)
        target = pl.ds(pl.multiple_of(k * BS, BS), BS)
        return [
            pltpu.make_async_copy(
                halves.at[k & 1, h, :, lanes], out.at[i, target, :], out_sems.at[k & 1, h]
            )
            for h, out in enumerate((high, low))
        ]

    def drain(k):
        def one(i, c):
            for copy in outgoing(k, i):
                copy.wait()
            return c

        lax.fori_loop(0, subsets, one, 0)

    for k in range(3):
        fetch(jnp.int32(k))

    def step(k, c):
        fetch(k + 3)
        at, to = k & 3, k & 1
        r = plan[z.at_rows + s * z.row_room + k]

        @pl.when(k < rows)
        def _():
            def arrived(t, c):
                pltpu.make_async_copy(window.at[:BS, :BS], blocks.at[at, t], in_sems.at[at]).wait()
                return c

            lax.fori_loop(0, cols, arrived, 0)

        @pl.when(k >= 2)
        def _():
            drain(k - 2)

        def fill(t, c):
            cb = plan[z.at_cols + s * z.col_room + t]
            keep = jnp.logical_and(k < rows, pattern[r * z.col_blocks + cb] > 0)
            block = jnp.where(keep, blocks[at, t], 0.0)
            span = pl.ds(pl.multiple_of(t * BS, BS), BS)
            top = block.astype(BF16)
            halves[to, 0, :, span] = top
            halves[to, 1, :, span] = (block - top.astype(F32)).astype(BF16)
            return c

        lax.fori_loop(0, cols, fill, 0)

        def pad(t, c):
            span = pl.ds(pl.multiple_of(t * BS, BS), BS)
            halves[to, 0, :, span] = jnp.zeros((BS, BS), BF16)
            halves[to, 1, :, span] = jnp.zeros((BS, BS), BF16)
            return c

        lax.fori_loop(cols, subsets * z.slot, pad, 0)

        def send(i, c):
            for copy in outgoing(k, i):
                copy.start()
            return c

        lax.fori_loop(0, subsets, send, 0)
        return c

    lax.fori_loop(0, steps, step, 0)
    for back in (2, 1):
        @pl.when(steps >= back)
        def _(back=back):
            drain(steps - back)


def pack_window(z, far, plan, pattern, window):
    smem = pl.BlockSpec(memory_space=pltpu.SMEM)
    anywhere = pl.BlockSpec(memory_space=pl.ANY)
    shape = jax.ShapeDtypeStruct((z.prow, z.deep * BS, z.lanes), BF16)
    return pl.pallas_call(
        functools.partial(pack_body, z, far),
        out_shape=(shape, shape),
        in_specs=[smem, smem, anywhere],
        out_specs=(anywhere, anywhere),
        scratch_shapes=[
            pltpu.VMEM((4, z.col_cap, BS, BS), F32),
            pltpu.VMEM((2, 2, BS, z.col_cap * BS), BF16),
            pltpu.SemaphoreType.DMA((4,)),
            pltpu.SemaphoreType.DMA((2, 2)),
        ],
        compiler_params=pltpu.CompilerParams(vmem_limit_bytes=VMEM_BYTES),
        cost_estimate=pl.CostEstimate(
            flops=0, transcendentals=0, bytes_accessed=z.deep * BS * z.col_cap * BS * 8
        ),
        name="pack_window",
    )(plan, pattern, window)


def product_body(z, far, reach, plan, *refs):
    names = [0] if 0 in reach else []
    for d in reach:
        if d > 0:
            names += [-d, d]
    count = 2 * len(names)
    sources = {step: (refs[2 * k], refs[2 * k + 1]) for k, step in enumerate(names)}
    packed = refs[count : count + 2]
    sums = refs[count + 2 : count + 2 + z.prow]
    raw, top, rest, total, ring, sems, ring_sems = refs[count + 2 + z.prow :]
    p, j = lax.axis_index("prow"), lax.axis_index("pcol")
    s, plane, core = supernode(z, far), j // 2, j % 2
    per = z.planes // 2
    for qi in range(per):
        away = s * per + qi - plane
        for c in range(2):
            slot = qi * 2 + c
            for step, pair in sources.items():
                for k in range(2):
                    @pl.when(jnp.logical_and(away == step, (c == core) == (k == 0)))
                    def _(pair=pair, k=k, slot=slot):
                        pltpu.make_async_copy(pair[k], raw.at[slot], sems.at[slot]).start()

    cols = plan[z.at_count + 2 + s]
    depth = (plan[z.at_count + s] + DEPTH - 1) // DEPTH
    subsets = jnp.where(depth > 0, (cols + z.slot - 1) // z.slot, 0)
    jobs = subsets * depth

    def fetch(i, k, at):
        rows = pl.ds(pl.multiple_of(k * DEPTH * BS, DEPTH * BS), DEPTH * BS)
        return [
            pltpu.make_async_copy(packed[h].at[i, rows, :], ring.at[at, h], ring_sems.at[at, h])
            for h in range(2)
        ]

    def request(n, i, k, at):
        @pl.when(n < jobs)
        def _():
            for copy in fetch(i, k, at):
                copy.start()

        turn = k + 1 == depth
        return jnp.where(turn, i + 1, i), jnp.where(turn, 0, k + 1), jnp.where(at + 1 == RING, 0, at + 1)

    ahead = (jnp.int32(0), jnp.int32(0), jnp.int32(0))
    for n in range(RING - 1):
        ahead = request(n, *ahead)

    any_source = next(iter(sources.values()))[0]
    for slot in range(z.half):
        pltpu.make_async_copy(any_source, raw.at[slot], sems.at[slot]).wait()
        for level in range(2):
            rows = slice(level * BS + slot * z.thin, level * BS + (slot + 1) * z.thin)
            value = raw[slot, level]
            head = value.astype(BF16)
            top[rows, : z.row_cap * BS] = head
            rest[rows, : z.row_cap * BS] = (value - head.astype(F32)).astype(BF16)
            if z.deep > z.row_cap:
                blank = jnp.zeros((z.thin, (z.deep - z.row_cap) * BS), BF16)
                top[rows, z.row_cap * BS :] = blank
                rest[rows, z.row_cap * BS :] = blank
    for d in range(z.prow):
        @pl.when((p ^ d) >= subsets)
        def _(d=d):
            sums[d][...] = jnp.zeros_like(sums[d])

    def one_subset(i, carry):
        def one_depth(k, carry):
            n, at, ahead = carry
            ahead = request(n + RING - 1, *ahead)
            for copy in fetch(i, k, at):
                copy.wait()
            span = pl.ds(pl.multiple_of(k * DEPTH * BS, DEPTH * BS), DEPTH * BS)
            x_top, x_rest = top[:, span], rest[:, span]
            part = (
                jnp.dot(x_top, ring[at, 1], preferred_element_type=F32)
                + jnp.dot(x_rest, ring[at, 0], preferred_element_type=F32)
                + jnp.dot(x_top, ring[at, 0], preferred_element_type=F32)
            )

            @pl.when(k == 0)
            def _():
                total[...] = part

            @pl.when(k > 0)
            def _():
                total[...] += part

            return n + 1, jnp.where(at + 1 == RING, 0, at + 1), ahead

        carry = lax.fori_loop(0, depth, one_depth, carry)
        for d in range(z.prow):
            @pl.when((i ^ p) == d)
            def _(d=d):
                sums[d][...] = total[...]

        return carry

    lax.fori_loop(0, subsets, one_subset, (jnp.int32(0), jnp.int32(0), ahead))


def product(z, far, reach, plan, streams, packed):
    arrays = []
    if 0 in reach:
        arrays += list(streams[0])
    for d in reach:
        if d > 0:
            arrays += list(streams[-d]) + list(streams[d])
    smem = pl.BlockSpec(memory_space=pltpu.SMEM)
    vmem = pl.BlockSpec(memory_space=pltpu.VMEM)
    anywhere = pl.BlockSpec(memory_space=pl.ANY)
    shape = jax.ShapeDtypeStruct((2 * BS, z.lanes), F32)
    out = pl.pallas_call(
        functools.partial(product_body, z, far, reach),
        out_shape=(shape,) * z.prow,
        in_specs=[smem] + [anywhere] * (len(arrays) + 2),
        out_specs=(vmem,) * z.prow,
        scratch_shapes=[
            pltpu.VMEM((z.half, 2, z.thin, z.wide), F32),
            pltpu.VMEM((2 * BS, z.deep * BS), BF16),
            pltpu.VMEM((2 * BS, z.deep * BS), BF16),
            pltpu.VMEM((2 * BS, z.lanes), F32),
            pltpu.VMEM((RING, 2, DEPTH * BS, z.lanes), BF16),
            pltpu.SemaphoreType.DMA((z.half,)),
            pltpu.SemaphoreType.DMA((RING, 2)),
        ],
        compiler_params=pltpu.CompilerParams(vmem_limit_bytes=VMEM_BYTES),
        cost_estimate=pl.CostEstimate(
            flops=6 * 2 * BS * z.row_cap * BS * z.col_cap * BS,
            transcendentals=0,
            bytes_accessed=z.deep * BS * z.col_cap * BS * 4,
        ),
        name="window_product",
    )(plan, *arrays, *packed)
    return list(out)


def plain(left, right):
    return jnp.dot(left, right, precision=exact_mode, preferred_element_type=F32)


def across(left, right):
    return lax.dot_general(
        left, right, (((1,), (1,)), ((), ())), precision=exact_mode, preferred_element_type=F32
    )


def finish_body(z, plan, *refs):
    n = z.prow
    near_sum, far_sum = refs[:n], refs[n : 2 * n]
    kept, got = refs[2 * n], refs[2 * n + 1]
    routed = refs[2 * n + 2 : 2 * n + 1 + z.planes]
    corners = refs[2 * n + 1 + z.planes]
    outs = refs[2 * n + 2 + z.planes : 4 * n + 2 + z.planes]
    image, live, tails, done, small = refs[4 * n + 2 + z.planes :]
    p, j = lax.axis_index("prow"), lax.axis_index("pcol")
    plane, core = j // 2, j % 2
    near = supernode(z, False)
    for s, sums in ((near, near_sum), (1 - near, far_sum)):
        image[s] = functools.reduce(lambda a, b: a + b, [r[...] for r in sums])
    for step in range(z.planes):
        for k in range(2):
            shard = (kept, got)[k].at[0] if step == 0 else routed[step - 1].at[k]
            owner = 2 * (plane ^ step) + (core ^ k)
            s, slot = owner // z.half, owner % z.half
            for level in range(2):
                live[s, pl.ds(pl.multiple_of(level * BS + slot * z.thin, z.thin), z.thin), :] = shard[
                    level, :, : z.lanes
                ]
                tails[pl.ds(pl.multiple_of(owner * z.thin, z.thin), z.thin), level * BS : (level + 1) * BS] = shard[
                    level, :, z.lanes :
                ]
    first = jnp.logical_and(p == 0, j == 0)
    lane = lax.broadcasted_iota(jnp.int32, (1, z.lanes), 1) // BS + p * z.slot
    shared = lane < plan[z.at_count + 4]
    for s in range(2):
        other = 1 - s
        keep = jnp.zeros((1, z.lanes), F32)
        for t in range(z.slot):
            flag = plan[z.at_second + s * z.col_room + p * z.slot + t].astype(F32)
            keep = jnp.where(lane == p * z.slot + t, flag, keep)
        own_first = image[s, :BS, :]
        other_first = jnp.where(shared, image[other, :BS, :], 0.0)
        tail = tails[s * BS : (s + 1) * BS, :]
        second = (
            image[s, BS:, :]
            - plain(tail[:, s * BS : (s + 1) * BS], own_first)
            - plain(tail[:, other * BS : (other + 1) * BS], other_first)
        )
        done[s, 0] = -own_first
        done[s, 1] = -(second * keep)
        live_second = live[s, BS:, :]
        started = jnp.where(first, 1.0, 0.0)
        gram = across(own_first, live[s, :BS, :]) + started * corners[0, :, s * BS : (s + 1) * BS].T
        small[s * BS : (s + 1) * BS, :BS] = gram
        small[s * BS : (s + 1) * BS, BS : 2 * BS] = (
            across(second, live_second) + started * corners[1, :, s * BS : (s + 1) * BS].T
        )
        block = slice(2 * BS + s * BS, 2 * BS + (s + 1) * BS)
        crossed = plain(tails[:, s * BS : (s + 1) * BS], gram)
        small[s * BS : (s + 1) * BS, block] = crossed[s * BS : (s + 1) * BS] - across(live_second, own_first)
        small[other * BS : (other + 1) * BS, block] = crossed[other * BS : (other + 1) * BS] - across(
            jnp.where(shared, live[other, BS:, :], 0.0), own_first
        )
    for s in range(2):
        rows = slice(s * BS, (s + 1) * BS)
        small[rows, BS : 2 * BS] += across(small[rows, 2 * BS :], tails[rows, :])
    per = n // 2
    for d in range(n):
        q = p ^ d
        s, h = q // per, q % per
        for level in range(2):
            outs[d][level] = done[s, level, pl.ds(pl.multiple_of(h * z.piece, z.piece), z.piece), :]
            outs[n + d][level] = small[
                pl.ds(pl.multiple_of(q * z.piece, z.piece), z.piece), level * 2 * BS : (level + 1) * 2 * BS
            ]


def finish(z, plan, arrays, corners):
    smem = pl.BlockSpec(memory_space=pltpu.SMEM)
    vmem = pl.BlockSpec(memory_space=pltpu.VMEM)
    out = pl.pallas_call(
        functools.partial(finish_body, z),
        out_shape=(jax.ShapeDtypeStruct((2, z.piece, z.lanes), F32),) * z.prow
        + (jax.ShapeDtypeStruct((2, z.piece, 2 * BS), F32),) * z.prow,
        in_specs=[smem] + [vmem] * (len(arrays) + 1),
        out_specs=(vmem,) * (2 * z.prow),
        scratch_shapes=[
            pltpu.VMEM((2, 2 * BS, z.lanes), F32),
            pltpu.VMEM((2, 2 * BS, z.lanes), F32),
            pltpu.VMEM((2 * BS, 2 * BS), F32),
            pltpu.VMEM((2, 2, BS, z.lanes), F32),
            pltpu.VMEM((2 * BS, 4 * BS), F32),
        ],
        compiler_params=pltpu.CompilerParams(vmem_limit_bytes=VMEM_BYTES),
        name="finish_levels",
    )(plan, *arrays, corners)
    return out[: z.prow], out[z.prow :]


def spread_body(z, plan, *refs):
    n = z.prow
    parts, panels = refs[:n], refs[n]
    p = lax.axis_index("prow")
    s = p // (n // 2)
    for cb in range(z.col_blocks):
        span = slice(cb * BS, (cb + 1) * BS)
        at = plan[z.at_place + s * z.col_blocks + cb]
        owner = jnp.where(at < 0, -1, (jnp.maximum(at, 0) // z.slot) ^ p)
        lane = pl.ds(pl.multiple_of((jnp.maximum(at, 0) % z.slot) * BS, BS), BS)

        @pl.when(at < 0)
        def _():
            panels[:, :, span] = jnp.zeros((2, z.piece, BS), F32)

        for d in range(n):
            @pl.when(owner == d)
            def _(d=d):
                panels[:, :, span] = parts[d][:, :, lane]


def spread(z, plan, parts):
    smem = pl.BlockSpec(memory_space=pltpu.SMEM)
    vmem = pl.BlockSpec(memory_space=pltpu.VMEM)
    return pl.pallas_call(
        functools.partial(spread_body, z),
        out_shape=jax.ShapeDtypeStruct((2, z.piece, z.col_blocks * BS), F32),
        in_specs=[smem] + [vmem] * z.prow,
        out_specs=vmem,
        compiler_params=pltpu.CompilerParams(vmem_limit_bytes=VMEM_BYTES),
        cost_estimate=pl.CostEstimate(
            flops=0, transcendentals=0, bytes_accessed=4 * z.piece * z.col_blocks * BS * 4
        ),
        name="spread_panels",
    )(plan, *parts)


def settle_body(z, held, small, panels, diagonals, sem):
    del held
    small_ref = small
    diagonals[0] = small_ref[0, :, :BS]
    diagonals[1] = small_ref[0, :, BS:]

    @pl.when(lax.axis_index("pcol") == z.pcol - 1)
    def _():
        small_ref[1] = -small_ref[1]
        copy = pltpu.make_async_copy(
            small_ref.at[1], panels.at[1, :, pl.ds((z.col_blocks - 2) * BS, 2 * BS)], sem
        )
        copy.start()
        copy.wait()


def settle(z, panels, small):
    vmem = pl.BlockSpec(memory_space=pltpu.VMEM)
    anywhere = pl.BlockSpec(memory_space=pl.ANY)

    def body(held, small_in, panels_out, diagonals, scratch, sem):
        scratch[...] = small_in[...]
        settle_body(z, held, scratch, panels_out, diagonals, sem)

    return pl.pallas_call(
        body,
        out_shape=(
            jax.ShapeDtypeStruct(panels.shape, F32),
            jax.ShapeDtypeStruct((2, z.piece, BS), F32),
        ),
        in_specs=[anywhere, vmem],
        out_specs=(anywhere, vmem),
        scratch_shapes=[pltpu.VMEM((2, z.piece, 2 * BS), F32), pltpu.SemaphoreType.DMA],
        input_output_aliases={0: 0},
        compiler_params=pltpu.CompilerParams(vmem_limit_bytes=VMEM_BYTES),
        name="settle_corner",
    )(panels, small)


def whole_run(z, window, pattern, plan, own, thin_factor, corners):
    def twin(array, least, most):
        pairs = [(k, k ^ 1) for k in range(z.pcol) if least <= k // 2 <= most]
        return lax.ppermute(array, "pcol", pairs)

    def exchange(arrays):
        return [arrays[0]] + [
            lax.ppermute(arrays[d], "prow", [(k, k ^ d) for k in range(z.prow)]) for d in range(1, z.prow)
        ]

    last = z.planes - 1
    per = z.planes // 2
    packed = {}
    streams = {0: (own, twin(own, 0, last))}
    below, above = own, own
    for d in range(1, z.planes):
        below = lax.ppermute(below, "pcol", [(k, k + 2) for k in range(z.pcol - 2) if k // 2 >= d - 1])
        above = lax.ppermute(above, "pcol", [(k, k - 2) for k in range(2, z.pcol) if k // 2 <= last - d + 1])
        if d == 1:
            picked = pick(z, plan, thin_factor)
            plan_near, picked = lax.optimization_barrier((plan, list(picked)))
            picked = exchange(picked)
            packed[0] = pack_window(z, False, plan_near, pattern, window)
            below, above, packed[0] = lax.optimization_barrier((below, above, packed[0]))
        if d == 2:
            packed[1] = pack_window(z, True, plan, pattern, window)
            below, above, packed[1], picked = lax.optimization_barrier((below, above, packed[1], picked))
            keep, give = route(z, picked)
            got = twin(give, 0, last)
        if d == last:
            near_sum = product(z, False, range(per), plan, streams, packed[0])
            routed = jnp.stack([keep, got], axis=1)
            below, above, near_sum, routed = lax.optimization_barrier((below, above, near_sum, routed))
        streams[-d] = (below, twin(below, d, last))
        streams[d] = (above, twin(above, 0, last - d))

    near_sum = exchange(near_sum)
    routed = [
        lax.ppermute(routed[step], "pcol", [(c, c ^ (2 * step)) for c in range(z.pcol)])
        for step in range(1, z.planes)
    ]
    far_sum = exchange(product(z, True, range(1, z.planes), plan, streams, packed[1]))
    parts, small = finish(z, plan, near_sum + far_sum + [keep, got] + routed, corners)
    small = functools.reduce(lambda a, b: a + b, exchange(small))
    panels = spread(z, plan, exchange(parts))
    step = 1
    while step < z.pcol:
        small = small + lax.ppermute(small, "pcol", [(k, k ^ step) for k in range(z.pcol)])
        step *= 2
    return settle(z, panels, small)


def local(window, pattern, row_lists, factor, diag_inverse):
    prow, pcol = lax.axis_size("prow"), lax.axis_size("pcol")
    rows, cols = window.shape
    row_blocks, col_blocks = rows // BS, cols // BS
    thin_factor = jnp.swapaxes(factor, 1, 2)
    capacities = [
        (row_cap, up_to(col_cap, prow))
        for row_cap, col_cap in (
            (row_blocks // 2, 3 * col_blocks // 5),
            (3 * row_blocks // 5, 3 * col_blocks // 5),
            (3 * row_blocks // 5, 4 * col_blocks // 5),
            (row_blocks, col_blocks),
        )
    ]
    sizes = [
        Sizes(rows, cols, factor.shape[2], prow, pcol, row_lists.shape[2], row_cap, col_cap)
        for row_cap, col_cap in capacities
    ]
    plan, chosen, owns = make_plan(sizes[-1], capacities, row_lists, thin_factor)

    def branch(z, pattern, *rest):
        return whole_run(z, rest[0], pattern, plan, owns[z.row_cap], thin_factor, diag_inverse)

    panels, diagonals = lax.switch(
        chosen[0],
        [functools.partial(branch, z) for z in sizes],
        pattern.reshape(-1),
        window,
    )
    return jnp.swapaxes(panels, 1, 2), jnp.swapaxes(diagonals, 1, 2)


def solution(mesh):
    in_specs = (P("prow", "pcol"), P("prow", "pcol"), P(), P(None, "prow", "pcol"), P())
    out_specs = (P(None, "pcol", "prow"), P(None, None, "prow"))
    return jax.shard_map(local, mesh=mesh, in_specs=in_specs, out_specs=out_specs, check_vma=False)
```

```python
import functools

import jax
import jax.numpy as jnp
from jax import lax
from jax.experimental import pallas as pl
from jax.experimental.pallas import tpu as pltpu
from jax.sharding import PartitionSpec as P

BS = 128
DEPTH = 4
RING = 3
VMEM_BYTES = 60 * 1024 * 1024

F32 = jnp.float32
BF16 = jnp.bfloat16
exact_mode = lax.Precision.HIGHEST


def up_to(value, step):
    return (value + step - 1) // step * step


class Sizes:
    def __init__(self, rows, cols, thin, prow, pcol, listed, row_cap, col_cap):
        self.prow, self.pcol, self.planes = prow, pcol, pcol // 2
        self.share = pcol // prow
        self.thin, self.listed = thin, listed
        self.rows = rows
        self.row_blocks, self.col_blocks = rows // BS, cols // BS
        self.row_cap, self.col_cap = row_cap, col_cap
        self.deep = up_to(row_cap, DEPTH)
        self.wide = row_cap * BS
        self.slot = col_cap // prow
        self.lanes = self.slot * BS
        self.long = self.lanes + BS
        self.piece = 2 * BS // prow
        self.half = pcol // 2
        self.row_room = up_to(self.row_blocks, DEPTH) + 1
        self.col_room = up_to(self.col_blocks, prow) + 1
        at = 0
        for name, extent in (
            ("at_rows", 2 * self.row_room),
            ("at_cols", 2 * self.col_room),
            ("at_second", 2 * self.col_room),
            ("at_place", 2 * self.col_blocks),
            ("at_pick", self.share * self.col_room),
            ("at_count", 5),
        ):
            setattr(self, name, at)
            at += extent
        self.plan = at


def plan_body(z, capacities, row_caps, lists, thin_ref, plan, chosen, *refs):
    owns, (member, full, sem) = refs[: len(row_caps)], refs[len(row_caps) :]
    p, j = lax.axis_index("prow"), lax.axis_index("pcol")
    mine = 2 * j // z.pcol

    def clear(k, c):
        member[k] = 0
        return c

    lax.fori_loop(0, z.row_blocks * z.prow, clear, 0, unroll=8)

    def blank(k, c):
        plan[k] = 0
        return c

    lax.fori_loop(0, z.at_place, blank, 0, unroll=8)

    def wipe(k, c):
        plan[z.at_place + k] = -1
        return c

    lax.fori_loop(0, z.at_count - z.at_place, wipe, 0, unroll=8)
    for s in range(2):
        def mark(k, c, s=s):
            b = lists[0, s, k]
            member[b] = member[b] | (5 << s)
            return c

        lax.fori_loop(0, z.listed - 2, mark, 0, unroll=8)
        for k in range(z.listed - 2, z.listed):
            b = lists[0, s, k]
            member[b] = member[b] | (1 << s)

    def take_row(r, counts):
        v = member[p * z.row_blocks + r]
        for s in range(2):
            plan[z.at_rows + s * z.row_room + counts[s]] = r
        return tuple(counts[s] + ((v >> s) & 1) for s in range(2))

    row_counts = lax.fori_loop(0, z.row_blocks, take_row, (0, 0), unroll=4)

    def in_order(section, put):
        def take_both(cb, count):
            v = member[section * z.col_blocks + cb]

            @pl.when((v & 3) == 3)
            def _():
                for s in range(2):
                    put(s, count, cb, v)

            return count + ((v & 3) == 3).astype(jnp.int32)

        common = lax.fori_loop(0, z.col_blocks, take_both, 0, unroll=2)

        def take_one(cb, counts):
            v = member[section * z.col_blocks + cb]
            result = []
            for s in range(2):
                single = (v & 3) == (1 << s)

                @pl.when(single)
                def _(s=s):
                    put(s, counts[s], cb, v)

                result.append(counts[s] + single.astype(jnp.int32))
            return tuple(result)

        return lax.fori_loop(0, z.col_blocks, take_one, (common, common), unroll=2) + (common,)

    def put_col(s, t, cb, v):
        plan[z.at_cols + s * z.col_room + t] = cb
        plan[z.at_second + s * z.col_room + t] = (v >> (2 + s)) & 1
        plan[z.at_place + s * z.col_blocks + cb] = t

    for k, value in enumerate(row_counts + in_order(j, put_col)):
        plan[z.at_count + k] = value
    for r in range(z.share):
        def put_pick(s, t, cb, v, r=r):
            @pl.when(s == mine)
            def _():
                plan[z.at_pick + r * z.col_room + t] = 2 * (r * z.col_blocks + cb) + ((v >> (2 + s)) & 1)

        in_order(p * z.share + r, put_pick)

    most_rows, most_cols = 0, 0
    for q in range(z.prow):
        in_row = 0
        for r in range(z.share):
            section = q * z.share + r

            def tally(cb, c, section=section):
                v = member[section * z.col_blocks + cb]
                return c + (v & 1) + ((v & 2) << 15)

            in_col = lax.fori_loop(0, z.col_blocks, tally, 0, unroll=True)
            in_row = in_row + in_col
            most_cols = jnp.maximum(most_cols, jnp.maximum(in_col & 0xFFFF, in_col >> 16))
        most_rows = jnp.maximum(most_rows, jnp.maximum(in_row & 0xFFFF, in_row >> 16))
    tier = 0
    for row_cap, col_cap in capacities[:-1]:
        tier = tier + jnp.logical_or(most_rows > row_cap, most_cols > col_cap).astype(jnp.int32)
    chosen[0] = tier

    held = plan[z.at_count + mine]

    def pack(k, c):
        r = plan[z.at_rows + mine * z.row_room + k]
        second = (member[p * z.row_blocks + r] >> (2 + mine)) & 1
        source = pl.ds(pl.multiple_of(r * BS, BS), BS)
        target = pl.ds(pl.multiple_of(k * BS, BS), BS)
        full[0, :, target] = thin_ref[0, :, source]
        full[1, :, target] = jnp.where(second == 1, thin_ref[1, :, source], 0.0)
        return c

    lax.fori_loop(0, held, pack, 0)

    def pad(k, c):
        full[:, :, pl.ds(pl.multiple_of(k * BS, BS), BS)] = jnp.zeros((2, z.thin, BS), F32)
        return c

    lax.fori_loop(held, z.row_blocks, pad, 0)
    for row_cap, own in zip(row_caps, owns):
        wanted = functools.reduce(
            jnp.logical_or, [tier == k for k, pair in enumerate(capacities) if pair[0] == row_cap]
        )

        @pl.when(wanted)
        def _(row_cap=row_cap, own=own):
            copy = pltpu.make_async_copy(full.at[:, :, : row_cap * BS], own, sem)
            copy.start()
            copy.wait()


def make_plan(z, capacities, lists, thin_factor):
    row_caps = sorted({pair[0] for pair in capacities})
    smem = pl.BlockSpec(memory_space=pltpu.SMEM)
    vmem = pl.BlockSpec(memory_space=pltpu.VMEM)
    anywhere = pl.BlockSpec(memory_space=pl.ANY)
    plan, chosen, *owns = pl.pallas_call(
        functools.partial(plan_body, z, capacities, row_caps),
        out_shape=(jax.ShapeDtypeStruct((z.plan,), jnp.int32), jax.ShapeDtypeStruct((1,), jnp.int32))
        + tuple(jax.ShapeDtypeStruct((2, z.thin, cap * BS), F32) for cap in row_caps),
        in_specs=[smem, vmem],
        out_specs=(smem, smem) + (anywhere,) * len(row_caps),
        scratch_shapes=[
            pltpu.SMEM((z.row_blocks * z.prow,), jnp.int32),
            pltpu.VMEM((2, z.thin, z.row_blocks * BS), F32),
            pltpu.SemaphoreType.DMA,
        ],
        compiler_params=pltpu.CompilerParams(vmem_limit_bytes=VMEM_BYTES),
        name="plan_rows",
    )(lists, thin_factor)
    return plan, chosen, dict(zip(row_caps, owns))


def supernode(z, far):
    near = lax.axis_index("pcol") // z.half
    return 1 - near if far else near


def pick_body(z, plan, thin_ref, *outs):
    p = lax.axis_index("prow")
    for d in range(z.prow):
        for r in range(z.share):
            for t in range(z.slot):
                v = plan[z.at_pick + r * z.col_room + (p ^ d) * z.slot + t]
                span = slice(t * BS, (t + 1) * BS)
                source = pl.ds(pl.multiple_of((jnp.maximum(v, 0) >> 1) * BS, BS), BS)
                outs[d][r, 0, :, span] = jnp.where(v >= 0, thin_ref[0, :, source], 0.0)
                outs[d][r, 1, :, span] = jnp.where(
                    jnp.logical_and(v >= 0, (v & 1) == 1), thin_ref[1, :, source], 0.0
                )
            for q in range(2):
                outs[d][r, q, :, z.lanes :] = thin_ref[1, :, z.rows - (2 - q) * BS : z.rows - (1 - q) * BS]


def pick(z, plan, thin_factor):
    smem = pl.BlockSpec(memory_space=pltpu.SMEM)
    vmem = pl.BlockSpec(memory_space=pltpu.VMEM)
    return pl.pallas_call(
        functools.partial(pick_body, z),
        out_shape=(jax.ShapeDtypeStruct((z.share, 2, z.thin, z.long), F32),) * z.prow,
        in_specs=[smem, vmem],
        out_specs=(vmem,) * z.prow,
        compiler_params=pltpu.CompilerParams(vmem_limit_bytes=VMEM_BYTES),
        name="pick_blocks",
    )(plan, thin_factor)


def route_body(z, *refs):
    sources, (keep, give) = refs[: z.prow], refs[z.prow :]
    p, j = lax.axis_index("prow"), lax.axis_index("pcol")
    plane, core = j // 2, j % 2
    for step in range(z.planes):
        for d in range(z.prow):
            @pl.when((p ^ plane ^ step) == d)
            def _(step=step, d=d):
                keep[step, :, :, : z.lanes] = sources[d][core, :, :, : z.lanes]
                give[step, :, :, : z.lanes] = sources[d][1 - core, :, :, : z.lanes]

    for d in range(z.prow):
        @pl.when((p ^ d) == z.prow - 1)
        def _(d=d):
            for step in range(z.planes):
                keep[step, :, :, z.lanes :] = sources[d][0, :, :, z.lanes :]
                give[step, :, :, z.lanes :] = sources[d][0, :, :, z.lanes :]


def route(z, sources):
    vmem = pl.BlockSpec(memory_space=pltpu.VMEM)
    return pl.pallas_call(
        functools.partial(route_body, z),
        out_shape=(jax.ShapeDtypeStruct((z.planes, 2, z.thin, z.long), F32),) * 2,
        in_specs=[vmem] * z.prow,
        out_specs=(vmem, vmem),
        compiler_params=pltpu.CompilerParams(vmem_limit_bytes=VMEM_BYTES),
        name="route_blocks",
    )(*sources)


def pack_body(z, far, plan, pattern, window, packed, strips, halves, in_sems, out_sems):
    s = supernode(z, far)
    rows, cols = plan[z.at_count + s], plan[z.at_count + 2 + s]
    subsets = (cols + z.slot - 1) // z.slot
    steps = up_to(rows, DEPTH)

    def incoming(k):
        r = plan[z.at_rows + s * z.row_room + k]
        return pltpu.make_async_copy(
            window.at[pl.ds(pl.multiple_of(r * BS, BS), BS), :], strips.at[k & 3], in_sems.at[k & 3]
        )

    def outgoing(k, i):
        return pltpu.make_async_copy(
            halves.at[k & 1, :, :, i * z.lanes : (i + 1) * z.lanes],
            packed.at[:, i, pl.ds(pl.multiple_of(k * BS, BS), BS), :],
            out_sems.at[k & 1, i],
        )

    def fetch(k):
        @pl.when(k < rows)
        def _():
            incoming(k).start()

    def drain(k):
        for i in range(z.prow):
            @pl.when(i < subsets)
            def _(i=i):
                outgoing(k, i).wait()

    for k in range(3):
        fetch(jnp.int32(k))

    def step(k, c):
        fetch(k + 3)
        at, to = k & 3, k & 1
        r = plan[z.at_rows + s * z.row_room + k]

        @pl.when(k < rows)
        def _():
            incoming(k).wait()

        @pl.when(k >= 2)
        def _():
            drain(k - 2)

        for i in range(z.prow):
            @pl.when(i < subsets)
            def _(i=i):
                for t in range(i * z.slot, (i + 1) * z.slot):
                    cb = plan[z.at_cols + s * z.col_room + t]
                    stored = pattern[r * z.col_blocks + cb] > 0
                    keep = jnp.logical_and(jnp.logical_and(k < rows, t < cols), stored)
                    block = strips[at, :, pl.ds(pl.multiple_of(cb * BS, BS), BS)]
                    block = jnp.where(keep, block, 0.0)
                    span = slice(t * BS, (t + 1) * BS)
                    top = block.astype(BF16)
                    halves[to, 0, :, span] = top
                    halves[to, 1, :, span] = (block - top.astype(F32)).astype(BF16)
                outgoing(k, i).start()

        return c

    lax.fori_loop(0, steps, step, 0)
    for back in (2, 1):
        @pl.when(steps >= back)
        def _(back=back):
            drain(steps - back)


def pack_window(z, far, plan, pattern, window):
    smem = pl.BlockSpec(memory_space=pltpu.SMEM)
    anywhere = pl.BlockSpec(memory_space=pl.ANY)
    return pl.pallas_call(
        functools.partial(pack_body, z, far),
        out_shape=jax.ShapeDtypeStruct((2, z.prow, z.deep * BS, z.lanes), BF16),
        in_specs=[smem, smem, anywhere],
        out_specs=anywhere,
        scratch_shapes=[
            pltpu.VMEM((4, BS, z.col_blocks * BS), F32),
            pltpu.VMEM((2, 2, BS, z.col_cap * BS), BF16),
            pltpu.SemaphoreType.DMA((4,)),
            pltpu.SemaphoreType.DMA((2, z.prow)),
        ],
        compiler_params=pltpu.CompilerParams(vmem_limit_bytes=VMEM_BYTES),
        cost_estimate=pl.CostEstimate(
            flops=0, transcendentals=0, bytes_accessed=z.deep * BS * z.col_cap * BS * 8
        ),
        name="pack_window",
    )(plan, pattern, window)


def product_body(z, far, reach, plan, *refs):
    names = [0] if 0 in reach else []
    for d in reach:
        if d > 0:
            names += [-d, d]
    count = 2 * len(names)
    sources = {step: (refs[2 * k], refs[2 * k + 1]) for k, step in enumerate(names)}
    packed = refs[count]
    sums = refs[count + 1 : count + 1 + z.prow]
    raw, top, rest, total, ring, sems, ring_sems = refs[count + 1 + z.prow :]
    p, j = lax.axis_index("prow"), lax.axis_index("pcol")
    s, plane, core = supernode(z, far), j // 2, j % 2
    per = z.planes // 2
    for qi in range(per):
        away = s * per + qi - plane
        for c in range(2):
            slot = qi * 2 + c
            for step, pair in sources.items():
                for k in range(2):
                    @pl.when(jnp.logical_and(away == step, (c == core) == (k == 0)))
                    def _(pair=pair, k=k, slot=slot):
                        pltpu.make_async_copy(pair[k], raw.at[slot], sems.at[slot]).start()

    cols = plan[z.at_count + 2 + s]
    depth = (plan[z.at_count + s] + DEPTH - 1) // DEPTH
    subsets = jnp.where(depth > 0, (cols + z.slot - 1) // z.slot, 0)
    jobs = subsets * depth

    def fetch(i, k, at):
        rows = pl.ds(pl.multiple_of(k * DEPTH * BS, DEPTH * BS), DEPTH * BS)
        return pltpu.make_async_copy(packed.at[:, i, rows, :], ring.at[at], ring_sems.at[at])

    def request(n, i, k, at):
        @pl.when(n < jobs)
        def _():
            fetch(i, k, at).start()

        turn = k + 1 == depth
        return jnp.where(turn, i + 1, i), jnp.where(turn, 0, k + 1), jnp.where(at + 1 == RING, 0, at + 1)

    ahead = (jnp.int32(0), jnp.int32(0), jnp.int32(0))
    for n in range(RING - 1):
        ahead = request(n, *ahead)

    any_source = next(iter(sources.values()))[0]
    for slot in range(z.half):
        pltpu.make_async_copy(any_source, raw.at[slot], sems.at[slot]).wait()
        for level in range(2):
            rows = slice(level * BS + slot * z.thin, level * BS + (slot + 1) * z.thin)
            value = raw[slot, level]
            head = value.astype(BF16)
            top[rows, : z.row_cap * BS] = head
            rest[rows, : z.row_cap * BS] = (value - head.astype(F32)).astype(BF16)
            if z.deep > z.row_cap:
                blank = jnp.zeros((z.thin, (z.deep - z.row_cap) * BS), BF16)
                top[rows, z.row_cap * BS :] = blank
                rest[rows, z.row_cap * BS :] = blank
    for d in range(z.prow):
        @pl.when((p ^ d) >= subsets)
        def _(d=d):
            sums[d][...] = jnp.zeros_like(sums[d])

    def one_subset(i, carry):
        def one_depth(k, carry):
            n, at, ahead = carry
            ahead = request(n + RING - 1, *ahead)
            fetch(i, k, at).wait()
            span = pl.ds(pl.multiple_of(k * DEPTH * BS, DEPTH * BS), DEPTH * BS)
            x_top, x_rest = top[:, span], rest[:, span]
            part = (
                jnp.dot(x_top, ring[at, 1], preferred_element_type=F32)
                + jnp.dot(x_rest, ring[at, 0], preferred_element_type=F32)
                + jnp.dot(x_top, ring[at, 0], preferred_element_type=F32)
            )

            @pl.when(k == 0)
            def _():
                total[...] = part

            @pl.when(k > 0)
            def _():
                total[...] += part

            return n + 1, jnp.where(at + 1 == RING, 0, at + 1), ahead

        carry = lax.fori_loop(0, depth, one_depth, carry)
        for d in range(z.prow):
            @pl.when((i ^ p) == d)
            def _(d=d):
                sums[d][...] = total[...]

        return carry

    lax.fori_loop(0, subsets, one_subset, (jnp.int32(0), jnp.int32(0), ahead))


def product(z, far, reach, plan, streams, packed):
    arrays = []
    if 0 in reach:
        arrays += list(streams[0])
    for d in reach:
        if d > 0:
            arrays += list(streams[-d]) + list(streams[d])
    smem = pl.BlockSpec(memory_space=pltpu.SMEM)
    vmem = pl.BlockSpec(memory_space=pltpu.VMEM)
    anywhere = pl.BlockSpec(memory_space=pl.ANY)
    shape = jax.ShapeDtypeStruct((2 * BS, z.lanes), F32)
    out = pl.pallas_call(
        functools.partial(product_body, z, far, reach),
        out_shape=(shape,) * z.prow,
        in_specs=[smem] + [anywhere] * (len(arrays) + 1),
        out_specs=(vmem,) * z.prow,
        scratch_shapes=[
            pltpu.VMEM((z.half, 2, z.thin, z.wide), F32),
            pltpu.VMEM((2 * BS, z.deep * BS), BF16),
            pltpu.VMEM((2 * BS, z.deep * BS), BF16),
            pltpu.VMEM((2 * BS, z.lanes), F32),
            pltpu.VMEM((RING, 2, DEPTH * BS, z.lanes), BF16),
            pltpu.SemaphoreType.DMA((z.half,)),
            pltpu.SemaphoreType.DMA((RING,)),
        ],
        compiler_params=pltpu.CompilerParams(vmem_limit_bytes=VMEM_BYTES),
        cost_estimate=pl.CostEstimate(
            flops=6 * 2 * BS * z.row_cap * BS * z.col_cap * BS,
            transcendentals=0,
            bytes_accessed=z.deep * BS * z.col_cap * BS * 4,
        ),
        name="window_product",
    )(plan, *arrays, packed)
    return list(out)


def plain(left, right):
    return jnp.dot(left, right, precision=exact_mode, preferred_element_type=F32)


def across(left, right):
    return lax.dot_general(
        left, right, (((1,), (1,)), ((), ())), precision=exact_mode, preferred_element_type=F32
    )


def finish_body(z, plan, *refs):
    n = z.prow
    near_sum, far_sum = refs[:n], refs[n : 2 * n]
    kept, got = refs[2 * n], refs[2 * n + 1]
    routed = refs[2 * n + 2 : 2 * n + 1 + z.planes]
    corners = refs[2 * n + 1 + z.planes]
    outs = refs[2 * n + 2 + z.planes : 4 * n + 2 + z.planes]
    image, live, tails, done, small = refs[4 * n + 2 + z.planes :]
    p, j = lax.axis_index("prow"), lax.axis_index("pcol")
    plane, core = j // 2, j % 2
    near = supernode(z, False)
    for s, sums in ((near, near_sum), (1 - near, far_sum)):
        image[s] = functools.reduce(lambda a, b: a + b, [r[...] for r in sums])
    for step in range(z.planes):
        for k in range(2):
            shard = (kept, got)[k].at[0] if step == 0 else routed[step - 1].at[k]
            owner = 2 * (plane ^ step) + (core ^ k)
            s, slot = owner // z.half, owner % z.half
            for level in range(2):
                live[s, pl.ds(pl.multiple_of(level * BS + slot * z.thin, z.thin), z.thin), :] = shard[
                    level, :, : z.lanes
                ]
                tails[pl.ds(pl.multiple_of(owner * z.thin, z.thin), z.thin), level * BS : (level + 1) * BS] = shard[
                    level, :, z.lanes :
                ]
    first = jnp.logical_and(p == 0, j == 0)
    lane = lax.broadcasted_iota(jnp.int32, (1, z.lanes), 1) // BS + p * z.slot
    shared = lane < plan[z.at_count + 4]
    for s in range(2):
        other = 1 - s
        keep = jnp.zeros((1, z.lanes), F32)
        for t in range(z.slot):
            flag = plan[z.at_second + s * z.col_room + p * z.slot + t].astype(F32)
            keep = jnp.where(lane == p * z.slot + t, flag, keep)
        own_first = image[s, :BS, :]
        other_first = jnp.where(shared, image[other, :BS, :], 0.0)
        tail = tails[s * BS : (s + 1) * BS, :]
        second = (
            image[s, BS:, :]
            - plain(tail[:, s * BS : (s + 1) * BS], own_first)
            - plain(tail[:, other * BS : (other + 1) * BS], other_first)
        )
        done[s, 0] = -own_first
        done[s, 1] = -(second * keep)
        live_second = live[s, BS:, :]
        started = jnp.where(first, 1.0, 0.0)
        gram = across(own_first, live[s, :BS, :]) + started * corners[0, :, s * BS : (s + 1) * BS].T
        small[s * BS : (s + 1) * BS, :BS] = gram
        small[s * BS : (s + 1) * BS, BS : 2 * BS] = (
            across(second, live_second) + started * corners[1, :, s * BS : (s + 1) * BS].T
        )
        block = slice(2 * BS + s * BS, 2 * BS + (s + 1) * BS)
        crossed = plain(tails[:, s * BS : (s + 1) * BS], gram)
        small[s * BS : (s + 1) * BS, block] = crossed[s * BS : (s + 1) * BS] - across(live_second, own_first)
        small[other * BS : (other + 1) * BS, block] = crossed[other * BS : (other + 1) * BS] - across(
            jnp.where(shared, live[other, BS:, :], 0.0), own_first
        )
    for s in range(2):
        rows = slice(s * BS, (s + 1) * BS)
        small[rows, BS : 2 * BS] += across(small[rows, 2 * BS :], tails[rows, :])
    per = n // 2
    for d in range(n):
        q = p ^ d
        s, h = q // per, q % per
        for level in range(2):
            outs[d][level] = done[s, level, pl.ds(pl.multiple_of(h * z.piece, z.piece), z.piece), :]
            outs[n + d][level] = small[
                pl.ds(pl.multiple_of(q * z.piece, z.piece), z.piece), level * 2 * BS : (level + 1) * 2 * BS
            ]


def finish(z, plan, arrays, corners):
    smem = pl.BlockSpec(memory_space=pltpu.SMEM)
    vmem = pl.BlockSpec(memory_space=pltpu.VMEM)
    out = pl.pallas_call(
        functools.partial(finish_body, z),
        out_shape=(jax.ShapeDtypeStruct((2, z.piece, z.lanes), F32),) * z.prow
        + (jax.ShapeDtypeStruct((2, z.piece, 2 * BS), F32),) * z.prow,
        in_specs=[smem] + [vmem] * (len(arrays) + 1),
        out_specs=(vmem,) * (2 * z.prow),
        scratch_shapes=[
            pltpu.VMEM((2, 2 * BS, z.lanes), F32),
            pltpu.VMEM((2, 2 * BS, z.lanes), F32),
            pltpu.VMEM((2 * BS, 2 * BS), F32),
            pltpu.VMEM((2, 2, BS, z.lanes), F32),
            pltpu.VMEM((2 * BS, 4 * BS), F32),
        ],
        compiler_params=pltpu.CompilerParams(vmem_limit_bytes=VMEM_BYTES),
        name="finish_levels",
    )(plan, *arrays, corners)
    return out[: z.prow], out[z.prow :]


def spread_body(z, plan, *refs):
    n = z.prow
    parts, panels = refs[:n], refs[n]
    p = lax.axis_index("prow")
    s = p // (n // 2)
    for cb in range(z.col_blocks):
        span = slice(cb * BS, (cb + 1) * BS)
        at = plan[z.at_place + s * z.col_blocks + cb]
        owner = jnp.where(at < 0, -1, (jnp.maximum(at, 0) // z.slot) ^ p)
        lane = pl.ds(pl.multiple_of((jnp.maximum(at, 0) % z.slot) * BS, BS), BS)

        @pl.when(at < 0)
        def _():
            panels[:, :, span] = jnp.zeros((2, z.piece, BS), F32)

        for d in range(n):
            @pl.when(owner == d)
            def _(d=d):
                panels[:, :, span] = parts[d][:, :, lane]


def spread(z, plan, parts):
    smem = pl.BlockSpec(memory_space=pltpu.SMEM)
    vmem = pl.BlockSpec(memory_space=pltpu.VMEM)
    return pl.pallas_call(
        functools.partial(spread_body, z),
        out_shape=jax.ShapeDtypeStruct((2, z.piece, z.col_blocks * BS), F32),
        in_specs=[smem] + [vmem] * z.prow,
        out_specs=vmem,
        compiler_params=pltpu.CompilerParams(vmem_limit_bytes=VMEM_BYTES),
        cost_estimate=pl.CostEstimate(
            flops=0, transcendentals=0, bytes_accessed=4 * z.piece * z.col_blocks * BS * 4
        ),
        name="spread_panels",
    )(plan, *parts)


def settle_body(z, held, small, panels, diagonals, sem):
    del held
    small_ref = small
    diagonals[0] = small_ref[0, :, :BS]
    diagonals[1] = small_ref[0, :, BS:]

    @pl.when(lax.axis_index("pcol") == z.pcol - 1)
    def _():
        small_ref[1] = -small_ref[1]
        copy = pltpu.make_async_copy(
            small_ref.at[1], panels.at[1, :, pl.ds((z.col_blocks - 2) * BS, 2 * BS)], sem
        )
        copy.start()
        copy.wait()


def settle(z, panels, small):
    vmem = pl.BlockSpec(memory_space=pltpu.VMEM)
    anywhere = pl.BlockSpec(memory_space=pl.ANY)

    def body(held, small_in, panels_out, diagonals, scratch, sem):
        scratch[...] = small_in[...]
        settle_body(z, held, scratch, panels_out, diagonals, sem)

    return pl.pallas_call(
        body,
        out_shape=(
            jax.ShapeDtypeStruct(panels.shape, F32),
            jax.ShapeDtypeStruct((2, z.piece, BS), F32),
        ),
        in_specs=[anywhere, vmem],
        out_specs=(anywhere, vmem),
        scratch_shapes=[pltpu.VMEM((2, z.piece, 2 * BS), F32), pltpu.SemaphoreType.DMA],
        input_output_aliases={0: 0},
        compiler_params=pltpu.CompilerParams(vmem_limit_bytes=VMEM_BYTES),
        name="settle_corner",
    )(panels, small)


def whole_run(z, window, pattern, plan, own, thin_factor, corners):
    def twin(array, least, most):
        pairs = [(k, k ^ 1) for k in range(z.pcol) if least <= k // 2 <= most]
        return lax.ppermute(array, "pcol", pairs)

    def exchange(arrays):
        return [arrays[0]] + [
            lax.ppermute(arrays[d], "prow", [(k, k ^ d) for k in range(z.prow)]) for d in range(1, z.prow)
        ]

    def along(array, step):
        return lax.ppermute(array, "pcol", [(c, c ^ (2 * step)) for c in range(z.pcol)])

    hold = lax.optimization_barrier
    last = z.planes - 1
    per = z.planes // 2
    streams = {0: (own, twin(own, 0, last))}
    below, above = own, own
    for d in range(1, z.planes):
        below = lax.ppermute(below, "pcol", [(k, k + 2) for k in range(z.pcol - 2) if k // 2 >= d - 1])
        above = lax.ppermute(above, "pcol", [(k, k - 2) for k in range(2, z.pcol) if k // 2 <= last - d + 1])
        if d == 1:
            plan, picked = hold((plan, list(pick(z, plan, thin_factor))))
            picked = exchange(picked)
            packed_near = pack_window(z, False, plan, pattern, window)
            keep, give = route(z, picked)
            below, above, packed_near, keep, give = hold((below, above, packed_near, keep, give))
        if d == 2:
            got = twin(give, 0, last)
            packed_far = pack_window(z, True, plan, pattern, window)
            below, above, packed_far, got = hold((below, above, packed_far, got))
        if d == last:
            near_sum = product(z, False, range(per), plan, streams, packed_near)
            routed = jnp.stack([keep, got], axis=1)
            near_parts = exchange(near_sum)
            below, above, near_sum, routed = hold((below, above, near_sum, routed))
        streams[-d] = (below, twin(below, d, last))
        streams[d] = (above, twin(above, 0, last - d))

    sent = [along(routed[1], 1)]
    far_sum = product(z, True, range(1, z.planes), plan, streams, packed_far)
    far_sum, near_parts, sent, routed = hold((far_sum, near_parts, sent, routed))
    far_sum = exchange(far_sum)
    sent += [along(routed[step], step) for step in range(2, z.planes)]
    parts, small = finish(z, plan, near_parts + far_sum + [keep, got] + sent, corners)
    small = functools.reduce(lambda a, b: a + b, exchange(small))
    small = small + twin(small, 0, last)
    parts, small = hold((list(parts), small))
    panels = spread(z, plan, exchange(parts))
    step = 1
    while step < z.planes:
        small = small + along(small, step)
        step *= 2
    return settle(z, panels, small)


def local(window, pattern, row_lists, factor, diag_inverse):
    prow, pcol = lax.axis_size("prow"), lax.axis_size("pcol")
    rows, cols = window.shape
    row_blocks, col_blocks = rows // BS, cols // BS
    thin_factor = jnp.swapaxes(factor, 1, 2)
    capacities = [
        (row_cap, up_to(col_cap, prow))
        for row_cap, col_cap in (
            (row_blocks // 2, 3 * col_blocks // 5),
            (3 * row_blocks // 5, 4 * col_blocks // 5),
            (row_blocks, col_blocks),
        )
    ]
    sizes = [
        Sizes(rows, cols, factor.shape[2], prow, pcol, row_lists.shape[2], row_cap, col_cap)
        for row_cap, col_cap in capacities
    ]
    plan, chosen, owns = make_plan(sizes[-1], capacities, row_lists, thin_factor)

    def branch(z, pattern, *rest):
        return whole_run(z, rest[0], pattern, plan, owns[z.row_cap], thin_factor, diag_inverse)

    panels, diagonals = lax.switch(
        chosen[0],
        [functools.partial(branch, z) for z in sizes],
        pattern.reshape(-1),
        window,
    )
    return jnp.swapaxes(panels, 1, 2), jnp.swapaxes(diagonals, 1, 2)


def solution(mesh):
    in_specs = (P("prow", "pcol"), P("prow", "pcol"), P(), P(None, "prow", "pcol"), P())
    out_specs = (P(None, "pcol", "prow"), P(None, None, "prow"))
    return jax.shard_map(local, mesh=mesh, in_specs=in_specs, out_specs=out_specs, check_vma=False)
```

```python
import functools

import jax
import jax.numpy as jnp
from jax import lax
from jax.experimental import pallas as pl
from jax.experimental.pallas import tpu as pltpu
from jax.sharding import PartitionSpec as P

BS = 128
DEPTH = 4
RING = 3
VMEM_BYTES = 60 * 1024 * 1024

F32 = jnp.float32
BF16 = jnp.bfloat16
exact_mode = lax.Precision.HIGHEST


def up_to(value, step):
    return (value + step - 1) // step * step


class Sizes:
    def __init__(self, rows, cols, thin, prow, pcol, listed, row_cap, col_cap):
        self.prow, self.pcol, self.planes = prow, pcol, pcol // 2
        self.share = pcol // prow
        self.thin, self.listed = thin, listed
        self.rows = rows
        self.row_blocks, self.col_blocks = rows // BS, cols // BS
        self.row_cap, self.col_cap = row_cap, col_cap
        self.deep = up_to(row_cap, DEPTH)
        self.wide = row_cap * BS
        self.slot = col_cap // prow
        self.lanes = self.slot * BS
        self.long = self.lanes + BS
        self.piece = 2 * BS // prow
        self.half = pcol // 2
        self.row_room = up_to(self.row_blocks, DEPTH) + 1
        self.col_room = up_to(self.col_blocks, prow) + 1
        at = 0
        for name, extent in (
            ("at_rows", 2 * self.row_room),
            ("at_cols", 2 * self.col_room),
            ("at_second", 2 * self.col_room),
            ("at_place", 2 * self.col_blocks),
            ("at_pick", self.share * self.col_room),
            ("at_count", 5),
        ):
            setattr(self, name, at)
            at += extent
        self.plan = at


def plan_body(z, capacities, row_caps, lists, thin_ref, plan, chosen, *refs):
    owns, (member, full, sem) = refs[: len(row_caps)], refs[len(row_caps) :]
    p, j = lax.axis_index("prow"), lax.axis_index("pcol")
    mine = 2 * j // z.pcol

    def clear(k, c):
        member[k] = 0
        return c

    lax.fori_loop(0, z.row_blocks * z.prow, clear, 0, unroll=8)

    def blank(k, c):
        plan[k] = 0
        return c

    lax.fori_loop(0, z.at_place, blank, 0, unroll=8)

    def wipe(k, c):
        plan[z.at_place + k] = -1
        return c

    lax.fori_loop(0, z.at_count - z.at_place, wipe, 0, unroll=8)
    for s in range(2):
        def mark(k, c, s=s):
            b = lists[0, s, k]
            member[b] = member[b] | (5 << s)
            return c

        lax.fori_loop(0, z.listed - 2, mark, 0, unroll=8)
        for k in range(z.listed - 2, z.listed):
            b = lists[0, s, k]
            member[b] = member[b] | (1 << s)

    def take_row(r, counts):
        v = member[p * z.row_blocks + r]
        for s in range(2):
            plan[z.at_rows + s * z.row_room + counts[s]] = r
        return tuple(counts[s] + ((v >> s) & 1) for s in range(2))

    row_counts = lax.fori_loop(0, z.row_blocks, take_row, (0, 0), unroll=4)

    def in_order(section, put):
        def take_both(cb, count):
            v = member[section * z.col_blocks + cb]

            @pl.when((v & 3) == 3)
            def _():
                for s in range(2):
                    put(s, count, cb, v)

            return count + ((v & 3) == 3).astype(jnp.int32)

        common = lax.fori_loop(0, z.col_blocks, take_both, 0, unroll=2)

        def take_one(cb, counts):
            v = member[section * z.col_blocks + cb]
            result = []
            for s in range(2):
                single = (v & 3) == (1 << s)

                @pl.when(single)
                def _(s=s):
                    put(s, counts[s], cb, v)

                result.append(counts[s] + single.astype(jnp.int32))
            return tuple(result)

        return lax.fori_loop(0, z.col_blocks, take_one, (common, common), unroll=2) + (common,)

    def put_col(s, t, cb, v):
        plan[z.at_cols + s * z.col_room + t] = cb
        plan[z.at_second + s * z.col_room + t] = (v >> (2 + s)) & 1
        plan[z.at_place + s * z.col_blocks + cb] = t

    for k, value in enumerate(row_counts + in_order(j, put_col)):
        plan[z.at_count + k] = value
    for r in range(z.share):
        def put_pick(s, t, cb, v, r=r):
            @pl.when(s == mine)
            def _():
                plan[z.at_pick + r * z.col_room + t] = 2 * (r * z.col_blocks + cb) + ((v >> (2 + s)) & 1)

        in_order(p * z.share + r, put_pick)

    most_rows, most_cols = 0, 0
    for q in range(z.prow):
        in_row = 0
        for r in range(z.share):
            section = q * z.share + r

            def tally(cb, c, section=section):
                v = member[section * z.col_blocks + cb]
                return c + (v & 1) + ((v & 2) << 15)

            in_col = lax.fori_loop(0, z.col_blocks, tally, 0, unroll=True)
            in_row = in_row + in_col
            most_cols = jnp.maximum(most_cols, jnp.maximum(in_col & 0xFFFF, in_col >> 16))
        most_rows = jnp.maximum(most_rows, jnp.maximum(in_row & 0xFFFF, in_row >> 16))
    tier = 0
    for row_cap, col_cap in capacities[:-1]:
        tier = tier + jnp.logical_or(most_rows > row_cap, most_cols > col_cap).astype(jnp.int32)
    chosen[0] = tier

    held = plan[z.at_count + mine]

    def pack(k, c):
        r = plan[z.at_rows + mine * z.row_room + k]
        second = (member[p * z.row_blocks + r] >> (2 + mine)) & 1
        source = pl.ds(pl.multiple_of(r * BS, BS), BS)
        target = pl.ds(pl.multiple_of(k * BS, BS), BS)
        full[0, :, target] = thin_ref[0, :, source]
        full[1, :, target] = jnp.where(second == 1, thin_ref[1, :, source], 0.0)
        return c

    lax.fori_loop(0, held, pack, 0)

    def pad(k, c):
        full[:, :, pl.ds(pl.multiple_of(k * BS, BS), BS)] = jnp.zeros((2, z.thin, BS), F32)
        return c

    lax.fori_loop(held, z.row_blocks, pad, 0)
    for row_cap, own in zip(row_caps, owns):
        wanted = functools.reduce(
            jnp.logical_or, [tier == k for k, pair in enumerate(capacities) if pair[0] == row_cap]
        )

        @pl.when(wanted)
        def _(row_cap=row_cap, own=own):
            copy = pltpu.make_async_copy(full.at[:, :, : row_cap * BS], own, sem)
            copy.start()
            copy.wait()


def make_plan(z, capacities, lists, thin_factor):
    row_caps = sorted({pair[0] for pair in capacities})
    smem = pl.BlockSpec(memory_space=pltpu.SMEM)
    vmem = pl.BlockSpec(memory_space=pltpu.VMEM)
    anywhere = pl.BlockSpec(memory_space=pl.ANY)
    plan, chosen, *owns = pl.pallas_call(
        functools.partial(plan_body, z, capacities, row_caps),
        out_shape=(jax.ShapeDtypeStruct((z.plan,), jnp.int32), jax.ShapeDtypeStruct((1,), jnp.int32))
        + tuple(jax.ShapeDtypeStruct((2, z.thin, cap * BS), F32) for cap in row_caps),
        in_specs=[smem, vmem],
        out_specs=(smem, smem) + (anywhere,) * len(row_caps),
        scratch_shapes=[
            pltpu.SMEM((z.row_blocks * z.prow,), jnp.int32),
            pltpu.VMEM((2, z.thin, z.row_blocks * BS), F32),
            pltpu.SemaphoreType.DMA,
        ],
        compiler_params=pltpu.CompilerParams(vmem_limit_bytes=VMEM_BYTES),
        name="plan_rows",
    )(lists, thin_factor)
    return plan, chosen, dict(zip(row_caps, owns))


def supernode(z, far):
    near = lax.axis_index("pcol") // z.half
    return 1 - near if far else near


def pick_body(z, plan, thin_ref, *outs):
    p = lax.axis_index("prow")
    for d in range(z.prow):
        for r in range(z.share):
            for t in range(z.slot):
                v = plan[z.at_pick + r * z.col_room + (p ^ d) * z.slot + t]
                span = slice(t * BS, (t + 1) * BS)
                source = pl.ds(pl.multiple_of((jnp.maximum(v, 0) >> 1) * BS, BS), BS)
                outs[d][r, 0, :, span] = jnp.where(v >= 0, thin_ref[0, :, source], 0.0)
                outs[d][r, 1, :, span] = jnp.where(
                    jnp.logical_and(v >= 0, (v & 1) == 1), thin_ref[1, :, source], 0.0
                )
            for q in range(2):
                outs[d][r, q, :, z.lanes :] = thin_ref[1, :, z.rows - (2 - q) * BS : z.rows - (1 - q) * BS]


def pick(z, plan, thin_factor):
    smem = pl.BlockSpec(memory_space=pltpu.SMEM)
    vmem = pl.BlockSpec(memory_space=pltpu.VMEM)
    return pl.pallas_call(
        functools.partial(pick_body, z),
        out_shape=(jax.ShapeDtypeStruct((z.share, 2, z.thin, z.long), F32),) * z.prow,
        in_specs=[smem, vmem],
        out_specs=(vmem,) * z.prow,
        compiler_params=pltpu.CompilerParams(vmem_limit_bytes=VMEM_BYTES),
        name="pick_blocks",
    )(plan, thin_factor)


def route_body(z, *refs):
    sources, (keep, give) = refs[: z.prow], refs[z.prow :]
    p, j = lax.axis_index("prow"), lax.axis_index("pcol")
    plane, core = j // 2, j % 2
    for step in range(z.planes):
        for d in range(z.prow):
            @pl.when((p ^ plane ^ step) == d)
            def _(step=step, d=d):
                keep[step, :, :, : z.lanes] = sources[d][core, :, :, : z.lanes]
                give[step, :, :, : z.lanes] = sources[d][1 - core, :, :, : z.lanes]

    for d in range(z.prow):
        @pl.when((p ^ d) == z.prow - 1)
        def _(d=d):
            for step in range(z.planes):
                keep[step, :, :, z.lanes :] = sources[d][0, :, :, z.lanes :]
                give[step, :, :, z.lanes :] = sources[d][0, :, :, z.lanes :]


def route(z, sources):
    vmem = pl.BlockSpec(memory_space=pltpu.VMEM)
    return pl.pallas_call(
        functools.partial(route_body, z),
        out_shape=(jax.ShapeDtypeStruct((z.planes, 2, z.thin, z.long), F32),) * 2,
        in_specs=[vmem] * z.prow,
        out_specs=(vmem, vmem),
        compiler_params=pltpu.CompilerParams(vmem_limit_bytes=VMEM_BYTES),
        name="route_blocks",
    )(*sources)


def pack_body(z, far, plan, pattern, window, packed, strips, halves, in_sems, out_sems):
    s = supernode(z, far)
    rows, cols = plan[z.at_count + s], plan[z.at_count + 2 + s]
    subsets = (cols + z.slot - 1) // z.slot
    steps = up_to(rows, DEPTH)

    def incoming(k):
        r = plan[z.at_rows + s * z.row_room + k]
        return pltpu.make_async_copy(
            window.at[pl.ds(pl.multiple_of(r * BS, BS), BS), :], strips.at[k & 3], in_sems.at[k & 3]
        )

    def outgoing(k, i):
        return pltpu.make_async_copy(
            halves.at[k & 1, :, :, i * z.lanes : (i + 1) * z.lanes],
            packed.at[:, i, pl.ds(pl.multiple_of(k * BS, BS), BS), :],
            out_sems.at[k & 1, i],
        )

    def fetch(k):
        @pl.when(k < rows)
        def _():
            incoming(k).start()

    def drain(k):
        for i in range(z.prow):
            @pl.when(i < subsets)
            def _(i=i):
                outgoing(k, i).wait()

    for k in range(3):
        fetch(jnp.int32(k))

    def step(k, c):
        fetch(k + 3)
        at, to = k & 3, k & 1
        r = plan[z.at_rows + s * z.row_room + k]

        @pl.when(k < rows)
        def _():
            incoming(k).wait()

        @pl.when(k >= 2)
        def _():
            drain(k - 2)

        for i in range(z.prow):
            @pl.when(i < subsets)
            def _(i=i):
                for t in range(i * z.slot, (i + 1) * z.slot):
                    cb = plan[z.at_cols + s * z.col_room + t]
                    stored = pattern[r * z.col_blocks + cb] > 0
                    keep = jnp.logical_and(jnp.logical_and(k < rows, t < cols), stored)
                    block = strips[at, :, pl.ds(pl.multiple_of(cb * BS, BS), BS)]
                    block = jnp.where(keep, block, 0.0)
                    span = slice(t * BS, (t + 1) * BS)
                    top = block.astype(BF16)
                    halves[to, 0, :, span] = top
                    halves[to, 1, :, span] = (block - top.astype(F32)).astype(BF16)
                outgoing(k, i).start()

        return c

    lax.fori_loop(0, steps, step, 0)
    for back in (2, 1):
        @pl.when(steps >= back)
        def _(back=back):
            drain(steps - back)


def pack_window(z, far, plan, pattern, window):
    smem = pl.BlockSpec(memory_space=pltpu.SMEM)
    anywhere = pl.BlockSpec(memory_space=pl.ANY)
    return pl.pallas_call(
        functools.partial(pack_body, z, far),
        out_shape=jax.ShapeDtypeStruct((2, z.prow, z.deep * BS, z.lanes), BF16),
        in_specs=[smem, smem, anywhere],
        out_specs=anywhere,
        scratch_shapes=[
            pltpu.VMEM((4, BS, z.col_blocks * BS), F32),
            pltpu.VMEM((2, 2, BS, z.col_cap * BS), BF16),
            pltpu.SemaphoreType.DMA((4,)),
            pltpu.SemaphoreType.DMA((2, z.prow)),
        ],
        compiler_params=pltpu.CompilerParams(vmem_limit_bytes=VMEM_BYTES),
        cost_estimate=pl.CostEstimate(
            flops=0, transcendentals=0, bytes_accessed=z.deep * BS * z.col_cap * BS * 8
        ),
        name="pack_window",
    )(plan, pattern, window)


def product_body(z, far, reach, plan, *refs):
    names = [0] if 0 in reach else []
    for d in reach:
        if d > 0:
            names += [-d, d]
    count = 2 * len(names)
    sources = {step: (refs[2 * k], refs[2 * k + 1]) for k, step in enumerate(names)}
    packed = refs[count]
    sums = refs[count + 1 : count + 1 + z.prow]
    raw, top, rest, total, ring, sems, ring_sems = refs[count + 1 + z.prow :]
    p, j = lax.axis_index("prow"), lax.axis_index("pcol")
    s, plane, core = supernode(z, far), j // 2, j % 2
    per = z.planes // 2
    for qi in range(per):
        away = s * per + qi - plane
        for c in range(2):
            slot = qi * 2 + c
            for step, pair in sources.items():
                for k in range(2):
                    @pl.when(jnp.logical_and(away == step, (c == core) == (k == 0)))
                    def _(pair=pair, k=k, slot=slot):
                        pltpu.make_async_copy(pair[k], raw.at[slot], sems.at[slot]).start()

    cols = plan[z.at_count + 2 + s]
    depth = (plan[z.at_count + s] + DEPTH - 1) // DEPTH
    subsets = jnp.where(depth > 0, (cols + z.slot - 1) // z.slot, 0)
    jobs = subsets * depth

    def fetch(i, k, at):
        rows = pl.ds(pl.multiple_of(k * DEPTH * BS, DEPTH * BS), DEPTH * BS)
        return pltpu.make_async_copy(packed.at[:, i, rows, :], ring.at[at], ring_sems.at[at])

    def request(n, i, k, at):
        @pl.when(n < jobs)
        def _():
            fetch(i, k, at).start()

        turn = k + 1 == depth
        return jnp.where(turn, i + 1, i), jnp.where(turn, 0, k + 1), jnp.where(at + 1 == RING, 0, at + 1)

    ahead = (jnp.int32(0), jnp.int32(0), jnp.int32(0))
    for n in range(RING - 1):
        ahead = request(n, *ahead)

    any_source = next(iter(sources.values()))[0]
    for slot in range(z.half):
        pltpu.make_async_copy(any_source, raw.at[slot], sems.at[slot]).wait()
        for level in range(2):
            rows = slice(level * BS + slot * z.thin, level * BS + (slot + 1) * z.thin)
            value = raw[slot, level]
            head = value.astype(BF16)
            top[rows, : z.row_cap * BS] = head
            rest[rows, : z.row_cap * BS] = (value - head.astype(F32)).astype(BF16)
            if z.deep > z.row_cap:
                blank = jnp.zeros((z.thin, (z.deep - z.row_cap) * BS), BF16)
                top[rows, z.row_cap * BS :] = blank
                rest[rows, z.row_cap * BS :] = blank
    for d in range(z.prow):
        @pl.when((p ^ d) >= subsets)
        def _(d=d):
            sums[d][...] = jnp.zeros_like(sums[d])

    def one_subset(i, carry):
        def one_depth(k, carry):
            n, at, ahead = carry
            ahead = request(n + RING - 1, *ahead)
            fetch(i, k, at).wait()
            span = pl.ds(pl.multiple_of(k * DEPTH * BS, DEPTH * BS), DEPTH * BS)
            x_top, x_rest = top[:, span], rest[:, span]
            part = (
                jnp.dot(x_top, ring[at, 1], preferred_element_type=F32)
                + jnp.dot(x_rest, ring[at, 0], preferred_element_type=F32)
                + jnp.dot(x_top, ring[at, 0], preferred_element_type=F32)
            )

            @pl.when(k == 0)
            def _():
                total[...] = part

            @pl.when(k > 0)
            def _():
                total[...] += part

            return n + 1, jnp.where(at + 1 == RING, 0, at + 1), ahead

        carry = lax.fori_loop(0, depth, one_depth, carry)
        for d in range(z.prow):
            @pl.when((i ^ p) == d)
            def _(d=d):
                sums[d][...] = total[...]

        return carry

    lax.fori_loop(0, subsets, one_subset, (jnp.int32(0), jnp.int32(0), ahead))


def product(z, far, reach, plan, streams, packed):
    arrays = []
    if 0 in reach:
        arrays += list(streams[0])
    for d in reach:
        if d > 0:
            arrays += list(streams[-d]) + list(streams[d])
    smem = pl.BlockSpec(memory_space=pltpu.SMEM)
    vmem = pl.BlockSpec(memory_space=pltpu.VMEM)
    anywhere = pl.BlockSpec(memory_space=pl.ANY)
    shape = jax.ShapeDtypeStruct((2 * BS, z.lanes), F32)
    out = pl.pallas_call(
        functools.partial(product_body, z, far, reach),
        out_shape=(shape,) * z.prow,
        in_specs=[smem] + [anywhere] * (len(arrays) + 1),
        out_specs=(vmem,) * z.prow,
        scratch_shapes=[
            pltpu.VMEM((z.half, 2, z.thin, z.wide), F32),
            pltpu.VMEM((2 * BS, z.deep * BS), BF16),
            pltpu.VMEM((2 * BS, z.deep * BS), BF16),
            pltpu.VMEM((2 * BS, z.lanes), F32),
            pltpu.VMEM((RING, 2, DEPTH * BS, z.lanes), BF16),
            pltpu.SemaphoreType.DMA((z.half,)),
            pltpu.SemaphoreType.DMA((RING,)),
        ],
        compiler_params=pltpu.CompilerParams(vmem_limit_bytes=VMEM_BYTES),
        cost_estimate=pl.CostEstimate(
            flops=6 * 2 * BS * z.row_cap * BS * z.col_cap * BS,
            transcendentals=0,
            bytes_accessed=z.deep * BS * z.col_cap * BS * 4,
        ),
        name="window_product",
    )(plan, *arrays, packed)
    return list(out)


def plain(left, right):
    return jnp.dot(left, right, precision=exact_mode, preferred_element_type=F32)


def across(left, right):
    return lax.dot_general(
        left, right, (((1,), (1,)), ((), ())), precision=exact_mode, preferred_element_type=F32
    )


def finish_body(z, plan, *refs):
    n = z.prow
    near_sum, far_sum = refs[:n], refs[n : 2 * n]
    kept, got = refs[2 * n], refs[2 * n + 1]
    routed = refs[2 * n + 2 : 2 * n + 1 + z.planes]
    corners = refs[2 * n + 1 + z.planes]
    outs = refs[2 * n + 2 + z.planes : 4 * n + 2 + z.planes]
    image, live, tails, done, small = refs[4 * n + 2 + z.planes :]
    p, j = lax.axis_index("prow"), lax.axis_index("pcol")
    plane, core = j // 2, j % 2
    near = supernode(z, False)
    for s, sums in ((near, near_sum), (1 - near, far_sum)):
        image[s] = functools.reduce(lambda a, b: a + b, [r[...] for r in sums])
    for step in range(z.planes):
        for k in range(2):
            shard = (kept, got)[k].at[0] if step == 0 else routed[step - 1].at[k]
            owner = 2 * (plane ^ step) + (core ^ k)
            s, slot = owner // z.half, owner % z.half
            for level in range(2):
                live[s, pl.ds(pl.multiple_of(level * BS + slot * z.thin, z.thin), z.thin), :] = shard[
                    level, :, : z.lanes
                ]
                tails[pl.ds(pl.multiple_of(owner * z.thin, z.thin), z.thin), level * BS : (level + 1) * BS] = shard[
                    level, :, z.lanes :
                ]
    first = jnp.logical_and(p == 0, j == 0)
    lane = lax.broadcasted_iota(jnp.int32, (1, z.lanes), 1) // BS + p * z.slot
    shared = lane < plan[z.at_count + 4]
    for s in range(2):
        other = 1 - s
        keep = jnp.zeros((1, z.lanes), F32)
        for t in range(z.slot):
            flag = plan[z.at_second + s * z.col_room + p * z.slot + t].astype(F32)
            keep = jnp.where(lane == p * z.slot + t, flag, keep)
        own_first = image[s, :BS, :]
        other_first = jnp.where(shared, image[other, :BS, :], 0.0)
        tail = tails[s * BS : (s + 1) * BS, :]
        second = (
            image[s, BS:, :]
            - plain(tail[:, s * BS : (s + 1) * BS], own_first)
            - plain(tail[:, other * BS : (other + 1) * BS], other_first)
        )
        done[s, 0] = -own_first
        done[s, 1] = -(second * keep)
        live_second = live[s, BS:, :]
        started = jnp.where(first, 1.0, 0.0)
        gram = across(own_first, live[s, :BS, :]) + started * corners[0, :, s * BS : (s + 1) * BS].T
        small[s * BS : (s + 1) * BS, :BS] = gram
        small[s * BS : (s + 1) * BS, BS : 2 * BS] = (
            across(second, live_second) + started * corners[1, :, s * BS : (s + 1) * BS].T
        )
        block = slice(2 * BS + s * BS, 2 * BS + (s + 1) * BS)
        crossed = plain(tails[:, s * BS : (s + 1) * BS], gram)
        small[s * BS : (s + 1) * BS, block] = crossed[s * BS : (s + 1) * BS] - across(live_second, own_first)
        small[other * BS : (other + 1) * BS, block] = crossed[other * BS : (other + 1) * BS] - across(
            jnp.where(shared, live[other, BS:, :], 0.0), own_first
        )
    for s in range(2):
        rows = slice(s * BS, (s + 1) * BS)
        small[rows, BS : 2 * BS] += across(small[rows, 2 * BS :], tails[rows, :])
    per = n // 2
    for d in range(n):
        q = p ^ d
        s, h = q // per, q % per
        for level in range(2):
            outs[d][level] = done[s, level, pl.ds(pl.multiple_of(h * z.piece, z.piece), z.piece), :]
            outs[n + d][level] = small[
                pl.ds(pl.multiple_of(q * z.piece, z.piece), z.piece), level * 2 * BS : (level + 1) * 2 * BS
            ]


def finish(z, plan, arrays, corners):
    smem = pl.BlockSpec(memory_space=pltpu.SMEM)
    vmem = pl.BlockSpec(memory_space=pltpu.VMEM)
    out = pl.pallas_call(
        functools.partial(finish_body, z),
        out_shape=(jax.ShapeDtypeStruct((2, z.piece, z.lanes), F32),) * z.prow
        + (jax.ShapeDtypeStruct((2, z.piece, 2 * BS), F32),) * z.prow,
        in_specs=[smem] + [vmem] * (len(arrays) + 1),
        out_specs=(vmem,) * (2 * z.prow),
        scratch_shapes=[
            pltpu.VMEM((2, 2 * BS, z.lanes), F32),
            pltpu.VMEM((2, 2 * BS, z.lanes), F32),
            pltpu.VMEM((2 * BS, 2 * BS), F32),
            pltpu.VMEM((2, 2, BS, z.lanes), F32),
            pltpu.VMEM((2 * BS, 4 * BS), F32),
        ],
        compiler_params=pltpu.CompilerParams(vmem_limit_bytes=VMEM_BYTES),
        name="finish_levels",
    )(plan, *arrays, corners)
    return out[: z.prow], out[z.prow :]


def spread_body(z, plan, *refs):
    n = z.prow
    parts, panels = refs[:n], refs[n]
    p = lax.axis_index("prow")
    s = p // (n // 2)
    for cb in range(z.col_blocks):
        span = slice(cb * BS, (cb + 1) * BS)
        at = plan[z.at_place + s * z.col_blocks + cb]
        owner = jnp.where(at < 0, -1, (jnp.maximum(at, 0) // z.slot) ^ p)
        lane = pl.ds(pl.multiple_of((jnp.maximum(at, 0) % z.slot) * BS, BS), BS)

        @pl.when(at < 0)
        def _():
            panels[:, :, span] = jnp.zeros((2, z.piece, BS), F32)

        for d in range(n):
            @pl.when(owner == d)
            def _(d=d):
                panels[:, :, span] = parts[d][:, :, lane]


def spread(z, plan, parts):
    smem = pl.BlockSpec(memory_space=pltpu.SMEM)
    vmem = pl.BlockSpec(memory_space=pltpu.VMEM)
    return pl.pallas_call(
        functools.partial(spread_body, z),
        out_shape=jax.ShapeDtypeStruct((2, z.piece, z.col_blocks * BS), F32),
        in_specs=[smem] + [vmem] * z.prow,
        out_specs=vmem,
        compiler_params=pltpu.CompilerParams(vmem_limit_bytes=VMEM_BYTES),
        cost_estimate=pl.CostEstimate(
            flops=0, transcendentals=0, bytes_accessed=4 * z.piece * z.col_blocks * BS * 4
        ),
        name="spread_panels",
    )(plan, *parts)


def settle_body(z, held, small, panels, diagonals, sem):
    del held
    small_ref = small
    diagonals[0] = small_ref[0, :, :BS]
    diagonals[1] = small_ref[0, :, BS:]

    @pl.when(lax.axis_index("pcol") == z.pcol - 1)
    def _():
        small_ref[1] = -small_ref[1]
        copy = pltpu.make_async_copy(
            small_ref.at[1], panels.at[1, :, pl.ds((z.col_blocks - 2) * BS, 2 * BS)], sem
        )
        copy.start()
        copy.wait()


def settle(z, panels, small):
    vmem = pl.BlockSpec(memory_space=pltpu.VMEM)
    anywhere = pl.BlockSpec(memory_space=pl.ANY)

    def body(held, small_in, panels_out, diagonals, scratch, sem):
        scratch[...] = small_in[...]
        settle_body(z, held, scratch, panels_out, diagonals, sem)

    return pl.pallas_call(
        body,
        out_shape=(
            jax.ShapeDtypeStruct(panels.shape, F32),
            jax.ShapeDtypeStruct((2, z.piece, BS), F32),
        ),
        in_specs=[anywhere, vmem],
        out_specs=(anywhere, vmem),
        scratch_shapes=[pltpu.VMEM((2, z.piece, 2 * BS), F32), pltpu.SemaphoreType.DMA],
        input_output_aliases={0: 0},
        compiler_params=pltpu.CompilerParams(vmem_limit_bytes=VMEM_BYTES),
        name="settle_corner",
    )(panels, small)


def whole_run(z, window, pattern, plan, own, thin_factor, corners):
    def twin(array, least, most):
        pairs = [(k, k ^ 1) for k in range(z.pcol) if least <= k // 2 <= most]
        return lax.ppermute(array, "pcol", pairs)

    def exchange(arrays):
        return [arrays[0]] + [
            lax.ppermute(arrays[d], "prow", [(k, k ^ d) for k in range(z.prow)]) for d in range(1, z.prow)
        ]

    def along(array, step):
        return lax.ppermute(array, "pcol", [(c, c ^ (2 * step)) for c in range(z.pcol)])

    hold = lax.optimization_barrier
    last = z.planes - 1
    per = z.planes // 2
    streams = {0: (own, twin(own, 0, last))}
    below, above = own, own
    for d in range(1, z.planes):
        below = lax.ppermute(below, "pcol", [(k, k + 2) for k in range(z.pcol - 2) if k // 2 >= d - 1])
        above = lax.ppermute(above, "pcol", [(k, k - 2) for k in range(2, z.pcol) if k // 2 <= last - d + 1])
        if d == 1:
            plan, picked = hold((plan, list(pick(z, plan, thin_factor))))
            picked = exchange(picked)
            packed_near = pack_window(z, False, plan, pattern, window)
            keep, give = route(z, picked)
            below, above, packed_near, keep, give = hold((below, above, packed_near, keep, give))
        if d == 2:
            got = twin(give, 0, last)
            packed_far = pack_window(z, True, plan, pattern, window)
            below, above, packed_far, got = hold((below, above, packed_far, got))
        if d == last:
            near_sum = product(z, False, range(per), plan, streams, packed_near)
            routed = jnp.stack([keep, got], axis=1)
            near_parts = exchange(near_sum)
            below, above, near_sum, routed = hold((below, above, near_sum, routed))
        streams[-d] = (below, twin(below, d, last))
        streams[d] = (above, twin(above, 0, last - d))

    sent = [along(routed[step], step) for step in range(2, z.planes)]
    far_sum = product(z, True, range(1, z.planes), plan, streams, packed_far)
    far_sum, near_parts, routed = hold((far_sum, near_parts, routed))
    far_sum = exchange(far_sum)
    sent = [along(routed[1], 1)] + sent
    parts, small = finish(z, plan, near_parts + far_sum + [keep, got] + sent, corners)
    small = functools.reduce(lambda a, b: a + b, exchange(small))
    small = small + twin(small, 0, last)
    parts, small = hold((list(parts), small))
    panels = spread(z, plan, exchange(parts))
    step = 1
    while step < z.planes:
        small = small + along(small, step)
        step *= 2
    return settle(z, panels, small)


def local(window, pattern, row_lists, factor, diag_inverse):
    prow, pcol = lax.axis_size("prow"), lax.axis_size("pcol")
    rows, cols = window.shape
    row_blocks, col_blocks = rows // BS, cols // BS
    thin_factor = jnp.swapaxes(factor, 1, 2)
    capacities = [
        (row_cap, up_to(col_cap, prow))
        for row_cap, col_cap in (
            (row_blocks // 2, 3 * col_blocks // 5),
            (3 * row_blocks // 5, 4 * col_blocks // 5),
            (row_blocks, col_blocks),
        )
    ]
    sizes = [
        Sizes(rows, cols, factor.shape[2], prow, pcol, row_lists.shape[2], row_cap, col_cap)
        for row_cap, col_cap in capacities
    ]
    plan, chosen, owns = make_plan(sizes[-1], capacities, row_lists, thin_factor)

    def branch(z, pattern, *rest):
        return whole_run(z, rest[0], pattern, plan, owns[z.row_cap], thin_factor, diag_inverse)

    panels, diagonals = lax.switch(
        chosen[0],
        [functools.partial(branch, z) for z in sizes],
        pattern.reshape(-1),
        window,
    )
    return jnp.swapaxes(panels, 1, 2), jnp.swapaxes(diagonals, 1, 2)


def solution(mesh):
    in_specs = (P("prow", "pcol"), P("prow", "pcol"), P(), P(None, "prow", "pcol"), P())
    out_specs = (P(None, "pcol", "prow"), P(None, None, "prow"))
    return jax.shard_map(local, mesh=mesh, in_specs=in_specs, out_specs=out_specs, check_vma=False)
```
